256 devices in a mesh: blk: 64 (over z, x, y_hi), hid: 4 (over y_lo, core).
Axes of the slice: x: 4, y: 4 (y_hi: 2, y_lo: 2; y = y_hi * 2 + y_lo), z: 8, core: 2. Of those that a mesh axis runs over, the one named last changes fastest.
Arguments:
- inputs: bfloat16 [4096, 8192], P(None, 'blk'), may hold values from -6 to 6
- targets: bfloat16 [4096, 8192], P(None, 'blk'), may hold values from -6 to 6
- row_order: int32 [4096], replicated, may hold values from 0 to 4095, each once
- mix_order: int32 [128], replicated, may hold values from 0 to 127, each once
- first_factor: bfloat16 [64, 128, 128], P('blk'), may hold values from -0.5 to 0.5
- up_factor: bfloat16 [64, 448, 128], P('blk', 'hid'), may hold values from -0.5 to 0.5
- down_factor: bfloat16 [64, 448, 128], P('blk', 'hid'), may hold values from -0.25 to 0.25
- last_factor: bfloat16 [64, 128, 128], P('blk'), may hold values from -0.5 to 0.5
Outputs:
- grad_first: float32 [64, 128, 128], P('blk')
- grad_up: float32 [64, 448, 128], P('blk', 'hid')
- grad_down: float32 [64, 448, 128], P('blk', 'hid')
- grad_last: float32 [64, 128, 128], P('blk')
The draws below stay inside these ranges and needn't reach their ends.
Inputs may be any that keep to these rules, and one draw needn't show every extreme that they name: `row_order`: a permutation of the 4096 stored rows. `mix_order`: a permutation of the 128 features of a group.
All inputs are finite; a program needn't handle non-finite values.
Results may differ from the reference program's by a relative error of at most 0.018.
Values may be sent and summed in bfloat16 or wider, within the bound.
No kernel may reach another device: no remote copies, remote signals or barrier semaphores. Data moves between devices by JAX's collectives and lax.ppermute only.
A program may use at most 64 MiB of HBM per device.

```python
import math
import jax
import jax.numpy as jnp
from jax import lax

D = 8192
BS = 128
TOKENS = 4096
NB = 64
G = 2
HB = 448
N_HID = 4


def shard_levels(own_key, extent, cuts, least, largest):
    level, own = 1.0, jax.random.fold_in(own_key, 6)
    for axis_at, blocks in cuts:
        draws = jnp.exp(jax.random.uniform(jax.random.fold_in(own, axis_at), (blocks,), jnp.float32, least / len(cuts), largest / len(cuts)))
        level = level * jnp.repeat(draws, extent[axis_at] // blocks).reshape([-1 if axis == axis_at else 1 for axis in range(len(extent))])
    return level


def normal_values(rng, extent, spread, bound, shards=(), dtype=jnp.bfloat16):
    drawn = spread * jax.random.normal(rng, extent, jnp.float32)
    if shards:
        drawn = drawn * shard_levels(rng, extent, shards, -0.22, 0.18)
    return jnp.clip(drawn, -bound, bound).astype(dtype)


def setup_inputs(seed: int = 0) -> dict:
    keys = jax.random.split(jax.random.key(seed), 9)
    return {
        "inputs": normal_values(keys[0], (TOKENS, D), 1.0, 6.0, ((1, 64),)),
        "targets": normal_values(keys[1], (TOKENS, D), 1.0, 6.0, ((1, 64),)),
        "row_order": jax.random.permutation(keys[2], TOKENS).astype(jnp.int32),
        "mix_order": jax.random.permutation(keys[3], BS).astype(jnp.int32),
        "first_factor": normal_values(keys[4], (NB, BS, BS), BS ** -0.5, 0.5, ((0, 64),)),
        "up_factor": normal_values(keys[5], (NB, HB, BS), BS ** -0.5, 0.5, ((0, 64), (1, 4))),
        "down_factor": normal_values(keys[6], (NB, HB, BS), HB ** -0.5, 0.25, ((0, 64), (1, 4))),
        "last_factor": normal_values(keys[7], (NB, BS, BS), BS ** -0.5, 0.5, ((0, 64),)),
    }


def gelu_parts(preact):
    cdf = 0.5 * (1.0 + jax.scipy.special.erf(preact * (1.0 / math.sqrt(2.0))))
    dens = jnp.exp(-0.5 * preact * preact) * (1.0 / math.sqrt(2.0 * math.pi))
    return (preact * cdf, cdf + preact * dens)

def quarter_sum(values, weights, quarter):
    parts = jnp.einsum('tqh,qhc->qtc', values.reshape(values.shape[0], N_HID, quarter).astype(jnp.float32), weights.reshape(N_HID, quarter, weights.shape[1]).astype(jnp.float32))
    rounded = lax.optimization_barrier(parts.astype(jnp.bfloat16)).astype(jnp.float32)
    return lax.optimization_barrier(jnp.sum(rounded, axis=0)).astype(jnp.bfloat16)

def reference(inputs, targets, row_order, mix_order, first_factor, up_factor, down_factor, last_factor):
    quarter = HB // N_HID
    blocked = inputs.reshape(TOKENS, NB, BS)
    first_out = jnp.einsum('tkb,kbc->tkc', blocked.astype(jnp.float32), first_factor.astype(jnp.float32)).astype(jnp.bfloat16)
    grouped = first_out.reshape(TOKENS, NB, NB, G).transpose(0, 2, 1, 3).reshape(TOKENS, NB, BS)
    mixed = grouped[:, :, mix_order]
    mixed_by_group = mixed.transpose(1, 0, 2)

    def forward_group(items):
        group_in, up_block, down_block = items
        preact = jnp.dot(group_in, up_block.T, preferred_element_type=jnp.float32)
        hidden = gelu_parts(preact)[0].astype(jnp.bfloat16)
        return quarter_sum(hidden, down_block, quarter)
    summed = lax.map(forward_group, (mixed_by_group, up_factor, down_factor))
    returned = summed.reshape(NB, TOKENS, NB, G).transpose(1, 2, 0, 3).reshape(TOKENS, NB, BS)
    student = jnp.einsum('tkb,kbc->tkc', returned.astype(jnp.float32), last_factor.astype(jnp.float32))
    teacher = targets[row_order].reshape(TOKENS, NB, BS).astype(jnp.float32)
    err_grad = ((student - teacher) * (1.0 / math.sqrt(TOKENS))).astype(jnp.bfloat16)
    grad_last = jnp.einsum('tkb,tkc->kbc', returned.astype(jnp.float32), err_grad.astype(jnp.float32))
    grad_returned = jnp.einsum('tkc,kbc->tkb', err_grad.astype(jnp.float32), last_factor.astype(jnp.float32)).astype(jnp.bfloat16)
    grad_summed = grad_returned.reshape(TOKENS, NB, NB, G).transpose(2, 0, 1, 3).reshape(NB, TOKENS, BS)

    def backward_group(items):
        group_in, grad_out, up_block, down_block = items
        preact = jnp.dot(group_in, up_block.T, preferred_element_type=jnp.float32)
        hidden_full, slope = gelu_parts(preact)
        hidden = hidden_full.astype(jnp.bfloat16)
        down_grad = jnp.dot(hidden.T, grad_out, preferred_element_type=jnp.float32)
        grad_hidden = jnp.dot(grad_out, down_block.T, preferred_element_type=jnp.float32)
        grad_preact = (grad_hidden * slope).astype(jnp.bfloat16)
        up_grad = jnp.dot(grad_preact.T, group_in, preferred_element_type=jnp.float32)
        grad_in = quarter_sum(grad_preact, up_block, quarter)
        return (down_grad, up_grad, grad_in)
    grad_down, grad_up, grad_mixed = lax.map(backward_group, (mixed_by_group, grad_summed, up_factor, down_factor))
    inverse = jnp.argsort(mix_order).astype(jnp.int32)
    grad_grouped = grad_mixed[:, :, inverse]
    grad_first_out = grad_grouped.reshape(NB, TOKENS, NB, G).transpose(1, 2, 0, 3).reshape(TOKENS, NB, BS)
    grad_first = jnp.einsum('tkb,tkc->kbc', blocked.astype(jnp.float32), grad_first_out.astype(jnp.float32))
    return (grad_first, grad_up, grad_down, grad_last)
```

```python
import math

import jax
import jax.numpy as jnp
from jax import lax
from jax.sharding import PartitionSpec as P

BS = 128
NB = 64
G = 2
N_HID = 4


def gelu_parts(preact):
    cdf = 0.5 * (1.0 + jax.scipy.special.erf(preact * (1.0 / math.sqrt(2.0))))
    dens = jnp.exp(-0.5 * preact * preact) * (1.0 / math.sqrt(2.0 * math.pi))
    return (preact * cdf, cdf + preact * dens)


def token_groups():
    return [
        [b * N_HID + (q ^ (2 * (b % 2))) for b in range(NB)] for q in range(N_HID)
    ]


def from_partner(value, m):
    return lax.ppermute(value, "hid", [(i, i ^ m) for i in range(N_HID)])


def exchange(rows):
    pieces = rows.reshape(NB, 16, rows.shape[0] * rows.shape[1] // (NB * 16))
    pieces = lax.all_to_all(
        pieces, ("blk", "hid"), 0, 0, tiled=True, axis_index_groups=token_groups()
    )
    return pieces.reshape(rows.shape)


def dot(a, b, dims):
    return lax.dot_general(a, b, (dims, ((), ())), preferred_element_type=jnp.float32)


def sum_over_hid(part):
    got = [from_partner(part, m) for m in (1, 2, 3)]
    return (part + got[0]) + (got[1] + got[2])


def local(inputs, targets, row_order, mix_order, first_factor, up_factor, down_factor, last_factor):
    tokens = inputs.shape[0]
    count = tokens // N_HID
    loss_scale = 1.0 / math.sqrt(tokens)
    quarter = lax.axis_index("hid") ^ (2 * (lax.axis_index("blk") % 2))
    start = quarter * count
    x = lax.dynamic_slice_in_dim(inputs, start, count, 0)
    rows = lax.dynamic_slice_in_dim(row_order, start, count, 0)
    first = first_factor[0]
    last = last_factor[0]
    weights = jnp.stack([up_factor[0], down_factor[0]])
    gathered = [weights] + [from_partner(weights, m) for m in (1, 2, 3)]

    first_out = dot(first, x, ((0,), (1,))).astype(jnp.bfloat16)
    grouped = exchange(first_out)

    up = jnp.concatenate([g[0] for g in gathered])
    down = jnp.concatenate([g[1] for g in gathered])
    feature_ids = lax.broadcasted_iota(jnp.int32, (BS, BS), 0)
    one_hot = mix_order[None, :] == feature_ids
    up_mixed = dot(up, one_hot.astype(jnp.bfloat16), ((1,), (1,))).astype(jnp.bfloat16)
    teacher = jnp.take(targets, rows, axis=0)

    preact = dot(up_mixed, grouped, ((1,), (0,)))
    hidden_full, slope = gelu_parts(preact)
    hidden = hidden_full.astype(jnp.bfloat16)
    summed = dot(down, hidden, ((0,), (0,))).astype(jnp.bfloat16)
    returned = exchange(summed)

    student = dot(returned, last, ((0,), (0,)))
    err_grad = ((student - teacher.astype(jnp.float32)) * loss_scale).astype(jnp.bfloat16)
    grad_returned = dot(last, err_grad, ((1,), (1,))).astype(jnp.bfloat16)
    grad_summed = exchange(grad_returned)
    grad_last = dot(returned, err_grad, ((1,), (0,)))

    grad_hidden = dot(down, grad_summed, ((1,), (0,)))
    grad_preact = (grad_hidden * slope).astype(jnp.bfloat16)
    grad_grouped = dot(up_mixed, grad_preact, ((0,), (0,))).astype(jnp.bfloat16)
    grad_first_out = exchange(grad_grouped)

    grad_up = dot(grad_preact, grouped, ((1,), (1,)))
    grad_down = dot(hidden, grad_summed, ((1,), (1,)))
    both = jnp.stack([grad_up.reshape(N_HID, -1, BS), grad_down.reshape(N_HID, -1, BS)], 1)
    got = [both[0]] + [from_partner(both[m], m) for m in (1, 2, 3)]
    both = (got[0] + got[1]) + (got[2] + got[3])
    grad_up = jnp.dot(both[0], one_hot.astype(jnp.float32), precision=lax.Precision.HIGHEST)
    grad_down = both[1]
    grad_last = sum_over_hid(grad_last)

    grad_first = sum_over_hid(dot(x, grad_first_out, ((0,), (1,))))
    return (grad_first[None], grad_up[None], grad_down[None], grad_last[None])


def solution(mesh):
    placed = (
        P(None, "blk"),
        P(None, "blk"),
        P(),
        P(),
        P("blk", None, None),
        P("blk", "hid", None),
        P("blk", "hid", None),
        P("blk", None, None),
    )
    return jax.shard_map(
        local,
        mesh=mesh,
        in_specs=placed,
        out_specs=(
            P("blk", None, None),
            P("blk", "hid", None),
            P("blk", "hid", None),
            P("blk", None, None),
        ),
        check_vma=False,
    )
```

```python
import functools
import math

import jax
import jax.numpy as jnp
from jax import lax
from jax.experimental import pallas as pl
from jax.experimental.pallas import tpu as pltpu
from jax.sharding import PartitionSpec as P

BS = 128
NB = 64
N_HID = 4
LANES = 128
STEP = 256


def token_groups():
    return [
        [b * N_HID + (q ^ (2 * (b % 2))) for b in range(NB)] for q in range(N_HID)
    ]


def from_partner(value, m):
    return lax.ppermute(value, "hid", [(i, i ^ m) for i in range(N_HID)])


def exchange(rows):
    pieces = rows.reshape(NB, rows.shape[0] // NB, LANES)
    pieces = lax.all_to_all(
        pieces, ("blk", "hid"), 0, 0, tiled=True, axis_index_groups=token_groups()
    )
    return pieces.reshape(rows.shape)


def dot(a, b, dims):
    return lax.dot_general(a, b, (dims, ((), ())), preferred_element_type=jnp.float32)


def mm(a, b):
    return dot(a, b, ((1,), (0,)))


def sum_over_hid(part):
    got = [from_partner(part, m) for m in (1, 2, 3)]
    return (part + got[0]) + (got[1] + got[2])


def put_pieces(spread, value, at):
    chunks = spread.shape[0] // BS
    for j in range(value.shape[1] // LANES):
        spread[pl.ds(at // LANES + j, BS, chunks), :] = value[:, j * LANES : (j + 1) * LANES]


def get_pieces(spread, at, size):
    chunks = spread.shape[0] // BS
    parts = [spread[pl.ds(at // LANES + j, BS, chunks), :] for j in range(size // LANES)]
    return jnp.concatenate(parts, axis=1).astype(jnp.bfloat16)


def first_kernel(quarter_ref, x_ref, first_ref, out_ref, spread):
    del quarter_ref
    first_t = first_ref[0].T
    count = x_ref.shape[0]
    for at in range(0, count, STEP):
        put_pieces(spread, dot(first_t, x_ref[at : at + STEP, :], ((1,), (1,))), at)
    out_ref[...] = spread[...].astype(jnp.bfloat16)


def forward_kernel(in_ref, up_ref, down_t_ref, out_ref, hidden_ref, slope_ref, spread_in, spread):
    spread_in[...] = in_ref[...].astype(jnp.float32)
    up = up_ref[...]
    down_t = down_t_ref[...]
    for at in range(0, hidden_ref.shape[1], STEP):
        preact = mm(up, get_pieces(spread_in, at, STEP))
        cdf = 0.5 * (1.0 + lax.erf(preact * (1.0 / math.sqrt(2.0))))
        dens = jnp.exp(-0.5 * preact * preact) * (1.0 / math.sqrt(2.0 * math.pi))
        hidden = (preact * cdf).astype(jnp.bfloat16)
        hidden_ref[:, at : at + STEP] = hidden
        slope_ref[:, at : at + STEP] = cdf + preact * dens
        put_pieces(spread, mm(down_t, hidden), at)
    out_ref[...] = spread[...].astype(jnp.bfloat16)


def error_kernel(scale, in_ref, last_ref, teacher_ref, out_ref, err_ref, spread_in, spread):
    spread_in[...] = in_ref[...].astype(jnp.float32)
    last = last_ref[0]
    last_t = last.T
    for at in range(0, err_ref.shape[1], STEP):
        student = mm(last_t, get_pieces(spread_in, at, STEP))
        teacher = teacher_ref[:, at : at + STEP].astype(jnp.float32)
        err = ((student - teacher) * scale).astype(jnp.bfloat16)
        err_ref[:, at : at + STEP] = err
        put_pieces(spread, mm(last, err), at)
    out_ref[...] = spread[...].astype(jnp.bfloat16)


def backward_kernel(in_ref, down_ref, up_t_ref, slope_ref, out_ref, grad_ref, spread_in, spread):
    spread_in[...] = in_ref[...].astype(jnp.float32)
    down = down_ref[...]
    up_t = up_t_ref[...]
    for at in range(0, grad_ref.shape[1], STEP):
        grad_hidden = mm(down, get_pieces(spread_in, at, STEP))
        grad = (grad_hidden * slope_ref[:, at : at + STEP]).astype(jnp.bfloat16)
        grad_ref[:, at : at + STEP] = grad
        put_pieces(spread, mm(up_t, grad), at)
    out_ref[...] = spread[...].astype(jnp.bfloat16)


def last_kernel(in_ref, x_t_ref, out_ref, spread_in):
    spread_in[...] = in_ref[...].astype(jnp.float32)
    grad = get_pieces(spread_in, 0, x_t_ref.shape[1])
    out_ref[...] = dot(x_t_ref[...], grad, ((1,), (1,)))


def whole(n):
    return [pl.BlockSpec(memory_space=pltpu.VMEM)] * n


PARAMS = pltpu.CompilerParams(vmem_limit_bytes=16 * 1024 * 1024)


def call(kernel, ins, outs, spreads, rows, flops):
    moved = sum(a.size * a.dtype.itemsize for a in ins) + sum(
        math.prod(o.shape) * o.dtype.itemsize for o in outs
    )
    return pl.pallas_call(
        kernel,
        out_shape=outs,
        in_specs=whole(len(ins)),
        out_specs=whole(len(outs)),
        scratch_shapes=[pltpu.VMEM((rows, LANES), jnp.float32)] * spreads,
        compiler_params=PARAMS,
        cost_estimate=pl.CostEstimate(flops=flops, bytes_accessed=moved, transcendentals=0),
    )(*ins)


def local(inputs, targets, row_order, mix_order, first_factor, up_factor, down_factor, last_factor):
    tokens = inputs.shape[0]
    count = tokens // N_HID
    piece_rows = BS * count // LANES
    loss_scale = 1.0 / math.sqrt(tokens)
    quarter = lax.axis_index("hid") ^ (2 * (lax.axis_index("blk") % 2))
    start = quarter * count
    shape = jax.ShapeDtypeStruct
    pieces = shape((piece_rows, LANES), jnp.bfloat16)

    first_out = pl.pallas_call(
        first_kernel,
        out_shape=pieces,
        grid_spec=pltpu.PrefetchScalarGridSpec(
            num_scalar_prefetch=1,
            grid=(1,),
            in_specs=[
                pl.BlockSpec((count, BS), lambda i, q: (q[0], 0)),
                pl.BlockSpec((1, BS, BS), lambda i, q: (0, 0, 0)),
            ],
            out_specs=pl.BlockSpec((piece_rows, LANES), lambda i, q: (0, 0)),
            scratch_shapes=[pltpu.VMEM((piece_rows, LANES), jnp.float32)],
        ),
        compiler_params=PARAMS,
    )(quarter.astype(jnp.int32)[None], inputs, first_factor)
    up_factor, down_factor, first_out = lax.optimization_barrier((up_factor, down_factor, first_out))
    arrived = exchange(first_out)

    up = jnp.concatenate([up_factor[0]] + [from_partner(up_factor[0], m) for m in (1, 2, 3)])
    down = jnp.concatenate([down_factor[0]] + [from_partner(down_factor[0], m) for m in (1, 2, 3)])
    units = up.shape[0]
    feature_ids = lax.broadcasted_iota(jnp.int32, (BS, BS), 0)
    one_hot = mix_order[None, :] == feature_ids
    up_mixed = dot(up, one_hot.astype(jnp.bfloat16), ((1,), (1,))).astype(jnp.bfloat16)
    up_mixed_t = up_mixed.T
    down_t = down.T
    rows = lax.dynamic_slice_in_dim(row_order, start, count, 0)
    teacher_t = jnp.take(targets, rows, axis=0).T
    x_t = lax.dynamic_slice_in_dim(inputs, start, count, 0).T

    flops = 2 * units * BS * count
    summed, hidden, slope = call(
        forward_kernel,
        (arrived, up_mixed, down_t),
        (pieces, shape((units, count), jnp.bfloat16), shape((units, count), jnp.float32)),
        2, piece_rows, 2 * flops,
    )
    returned = exchange(summed)

    grad_returned, err_grad = call(
        functools.partial(error_kernel, loss_scale),
        (returned, last_factor, teacher_t),
        (pieces, shape((BS, count), jnp.bfloat16)),
        2, piece_rows, flops,
    )
    grad_arrived = exchange(grad_returned)

    grad_grouped, grad_preact = call(
        backward_kernel,
        (grad_arrived, down, up_mixed_t, slope),
        (pieces, shape((units, count), jnp.bfloat16)),
        2, piece_rows, 2 * flops,
    )
    grad_first_out = exchange(grad_grouped)

    grad_last = dot(returned.reshape(BS, count), err_grad, ((1,), (1,)))
    grad_up = dot(grad_preact, arrived.reshape(BS, count), ((1,), (1,)))
    grad_down = dot(hidden, grad_arrived.reshape(BS, count), ((1,), (1,)))
    both = jnp.stack([grad_up.reshape(N_HID, -1, BS), grad_down.reshape(N_HID, -1, BS)], 1)
    got = [both[0]] + [from_partner(both[m], m) for m in (1, 2, 3)]
    both = (got[0] + got[1]) + (got[2] + got[3])
    grad_up = jnp.dot(both[0], one_hot.astype(jnp.float32), precision=lax.Precision.HIGHEST)
    grad_down = both[1]
    grad_last = sum_over_hid(grad_last)

    (grad_first,) = call(
        last_kernel, (grad_first_out, x_t), (shape((BS, BS), jnp.float32),), 1, piece_rows, flops // 4
    )
    grad_first = sum_over_hid(grad_first)
    return (grad_first[None], grad_up[None], grad_down[None], grad_last[None])


def solution(mesh):
    placed = (
        P(None, "blk"),
        P(None, "blk"),
        P(),
        P(),
        P("blk", None, None),
        P("blk", "hid", None),
        P("blk", "hid", None),
        P("blk", None, None),
    )
    return jax.shard_map(
        local,
        mesh=mesh,
        in_specs=placed,
        out_specs=(
            P("blk", None, None),
            P("blk", "hid", None),
            P("blk", "hid", None),
            P("blk", None, None),
        ),
        check_vma=False,
    )
```

```python
import functools
import math

import jax
import jax.numpy as jnp
from jax import lax
from jax.experimental import pallas as pl
from jax.experimental.pallas import tpu as pltpu
from jax.sharding import PartitionSpec as P

BS = 128
NB = 64
N_HID = 4
LANES = 128
STEP = 256


def token_groups():
    return [
        [b * N_HID + (q ^ (2 * (b % 2))) for b in range(NB)] for q in range(N_HID)
    ]


def from_partner(value, m):
    return lax.ppermute(value, "hid", [(i, i ^ m) for i in range(N_HID)])


def exchange(rows):
    pieces = rows.reshape(NB, rows.shape[0] // NB, LANES)
    pieces = lax.all_to_all(
        pieces, ("blk", "hid"), 0, 0, tiled=True, axis_index_groups=token_groups()
    )
    return pieces.reshape(rows.shape)


def dot(a, b, dims):
    return lax.dot_general(a, b, (dims, ((), ())), preferred_element_type=jnp.float32)


def mm(a, b):
    return dot(a, b, ((1,), (0,)))


def sum_over_hid(part):
    got = [from_partner(part, m) for m in (1, 2, 3)]
    return (part + got[0]) + (got[1] + got[2])


def own_quarter():
    return lax.axis_index("hid") ^ (2 * (lax.axis_index("blk") % 2))


def put_pieces(spread, value, at):
    chunks = spread.shape[0] // BS
    for j in range(value.shape[1] // LANES):
        spread[pl.ds(at // LANES + j, BS, chunks), :] = value[:, j * LANES : (j + 1) * LANES]


def get_pieces(spread, at, size):
    chunks = spread.shape[0] // BS
    parts = [spread[pl.ds(at // LANES + j, BS, chunks), :] for j in range(size // LANES)]
    return jnp.concatenate(parts, axis=1).astype(jnp.bfloat16)


def keep(scratch, hbm, sems, i, size):
    columns = pl.ds(i * size, size)
    copy = pltpu.make_async_copy(scratch.at[:, columns], hbm.at[:, columns], sems.at[i])
    copy.start()
    return copy


def send_out(spread, buffer, hbm, sems, first_sem):
    half = spread.shape[0] // 2
    copies = []
    for i in range(2):
        rows = pl.ds(i * half, half)
        buffer[rows, :] = spread[rows, :].astype(jnp.bfloat16)
        copies.append(pltpu.make_async_copy(buffer.at[rows], hbm.at[rows], sems.at[first_sem + i]))
        copies[-1].start()
    return copies


def first_kernel(x_hbm, first_ref, out_hbm, x, spread, buffer, sems):
    count = x.shape[0]
    start = own_quarter() * count
    steps = count // STEP
    arrivals = []
    for i in range(steps):
        source = x_hbm.at[pl.ds(pl.multiple_of(start + i * STEP, STEP), STEP)]
        arrivals.append(pltpu.make_async_copy(source, x.at[pl.ds(i * STEP, STEP)], sems.at[i]))
        arrivals[-1].start()
    first_t = first_ref[0].T
    for i in range(steps):
        arrivals[i].wait()
        put_pieces(spread, dot(first_t, x[i * STEP : (i + 1) * STEP, :], ((1,), (1,))), i * STEP)
    for copy in send_out(spread, buffer, out_hbm, sems, steps):
        copy.wait()


def prepare_kernel(
    x_hbm, teacher_ref, mix_ref, *refs
):
    ups, downs = refs[0:4], refs[4:8]
    up_ref, up_t_ref, down_ref, down_t_ref, teacher_t_ref, x_t_ref, x, sem = refs[8:]
    count = x.shape[0]
    start = pl.multiple_of(own_quarter() * count, count)
    arrival = pltpu.make_async_copy(x_hbm.at[pl.ds(start, count)], x, sem)
    arrival.start()
    ids = lax.broadcasted_iota(jnp.int32, (BS, BS), 0)
    one_hot = (mix_ref[...] == ids).astype(jnp.float32).astype(jnp.bfloat16)
    eye = (lax.broadcasted_iota(jnp.int32, (BS, BS), 1) == ids).astype(jnp.float32)
    eye = eye.astype(jnp.bfloat16)
    up = jnp.concatenate([u[0] for u in ups])
    down = jnp.concatenate([d[0] for d in downs])
    down_ref[...] = down
    up_ref[...] = dot(up, one_hot, ((1,), (1,))).astype(jnp.bfloat16)
    up_t_ref[...] = dot(one_hot, up, ((1,), (1,))).astype(jnp.bfloat16)
    down_t_ref[...] = dot(eye, down, ((1,), (1,))).astype(jnp.bfloat16)
    teacher_t_ref[...] = dot(eye, teacher_ref[...], ((1,), (1,))).astype(jnp.bfloat16)
    arrival.wait()
    x_t_ref[...] = dot(eye, x[...], ((1,), (1,))).astype(jnp.bfloat16)


def forward_kernel(
    in_ref, up_ref, down_t_ref, out_ref, slope_ref, hidden_hbm, hidden_ref, spread_in, spread, sems
):
    spread_in[...] = in_ref[...].astype(jnp.float32)
    up = up_ref[...]
    down_t = down_t_ref[...]
    copies = []
    for i in range(hidden_ref.shape[1] // STEP):
        at = i * STEP
        preact = mm(up, get_pieces(spread_in, at, STEP))
        cdf = 0.5 * (1.0 + lax.erf(preact * (1.0 / math.sqrt(2.0))))
        dens = jnp.exp(-0.5 * preact * preact) * (1.0 / math.sqrt(2.0 * math.pi))
        hidden = (preact * cdf).astype(jnp.bfloat16)
        hidden_ref[:, at : at + STEP] = hidden
        copies.append(keep(hidden_ref, hidden_hbm, sems, i, STEP))
        slope_ref[:, at : at + STEP] = cdf + preact * dens
        put_pieces(spread, mm(down_t, hidden), at)
    out_ref[...] = spread[...].astype(jnp.bfloat16)
    for copy in copies:
        copy.wait()


def error_kernel(
    scale, in_ref, last_ref, teacher_ref, out_ref, err_hbm, err_ref, spread_in, spread, sems
):
    spread_in[...] = in_ref[...].astype(jnp.float32)
    last = last_ref[0]
    last_t = last.T
    copies = []
    for i in range(err_ref.shape[1] // STEP):
        at = i * STEP
        student = mm(last_t, get_pieces(spread_in, at, STEP))
        teacher = teacher_ref[:, at : at + STEP].astype(jnp.float32)
        err = ((student - teacher) * scale).astype(jnp.bfloat16)
        err_ref[:, at : at + STEP] = err
        copies.append(keep(err_ref, err_hbm, sems, i, STEP))
        put_pieces(spread, mm(last, err), at)
    out_ref[...] = spread[...].astype(jnp.bfloat16)
    for copy in copies:
        copy.wait()


def backward_kernel(
    in_ref, down_ref, up_t_ref, slope_ref, out_hbm, grad_hbm, grad_ref, spread_in, spread, buffer, sems
):
    spread_in[...] = in_ref[...].astype(jnp.float32)
    down = down_ref[...]
    up_t = up_t_ref[...]
    copies = []
    steps = grad_ref.shape[1] // STEP
    for i in range(steps):
        at = i * STEP
        grad_hidden = mm(down, get_pieces(spread_in, at, STEP))
        grad = (grad_hidden * slope_ref[:, at : at + STEP]).astype(jnp.bfloat16)
        grad_ref[:, at : at + STEP] = grad
        copies.append(keep(grad_ref, grad_hbm, sems, i, STEP))
        put_pieces(spread, mm(up_t, grad), at)
    for copy in copies + send_out(spread, buffer, out_hbm, sems, steps):
        copy.wait()


def weights_kernel(
    arrived_ref, returned_ref, grad_arrived_ref, hidden_ref, grad_ref, err_ref, mine_ref, theirs_ref, spread_in
):
    units, count = hidden_ref.shape
    half = units // 2

    def product(left, pieces_ref):
        spread_in[...] = pieces_ref[...].astype(jnp.float32)
        return dot(left, get_pieces(spread_in, 0, count), ((1,), (1,)))

    up = product(grad_ref[...], arrived_ref)
    mine_ref[0:half, :] = up[:half]
    theirs_ref[0:half, :] = up[half:]
    down = product(hidden_ref[...], grad_arrived_ref)
    mine_ref[half:units, :] = down[:half]
    theirs_ref[half:units, :] = down[half:]
    spread_in[...] = returned_ref[...].astype(jnp.float32)
    last = dot(get_pieces(spread_in, 0, count), err_ref[...], ((1,), (1,)))
    mine_ref[units:, :] = last
    theirs_ref[units:, :] = last


def chip_sum_kernel(mine_ref, got_ref, mine_out, theirs_out):
    quarter = (mine_ref.shape[0] - BS) // 4
    total = mine_ref[...] + got_ref[...]
    mine_out[0:quarter, :] = total[0:quarter]
    theirs_out[0:quarter, :] = total[quarter : 2 * quarter]
    mine_out[quarter : 2 * quarter, :] = total[2 * quarter : 3 * quarter]
    theirs_out[quarter : 2 * quarter, :] = total[3 * quarter : 4 * quarter]
    mine_out[2 * quarter :, :] = total[4 * quarter :]
    theirs_out[2 * quarter :, :] = total[4 * quarter :]


def totals_kernel(mine_ref, got_ref, mix_ref, up_ref, down_ref, last_ref):
    quarter = up_ref.shape[1]
    total = mine_ref[...] + got_ref[...]
    ids = lax.broadcasted_iota(jnp.int32, (BS, BS), 0)
    one_hot = (mix_ref[...] == ids).astype(jnp.float32)
    up_ref[0] = jnp.dot(
        total[0:quarter], one_hot, precision=lax.Precision.HIGHEST, preferred_element_type=jnp.float32
    )
    down_ref[0] = total[quarter : 2 * quarter]
    last_ref[0] = total[2 * quarter :]


def last_kernel(in_ref, x_t_ref, out_ref, spread_in):
    spread_in[...] = in_ref[...].astype(jnp.float32)
    grad = get_pieces(spread_in, 0, x_t_ref.shape[1])
    out_ref[...] = dot(x_t_ref[...], grad, ((1,), (1,)))


VMEM = pl.BlockSpec(memory_space=pltpu.VMEM)
HBM = pl.BlockSpec(memory_space=pltpu.HBM)
BF16 = jnp.bfloat16
F32 = jnp.float32


def call(kernel, ins, outs, scratch, flops, in_specs=None, out_specs=None):
    moved = sum(a.size * a.dtype.itemsize for a in ins) + sum(
        math.prod(o.shape) * o.dtype.itemsize for o in outs
    )
    return pl.pallas_call(
        kernel,
        out_shape=outs,
        in_specs=in_specs or [VMEM] * len(ins),
        out_specs=out_specs or [VMEM] * len(outs),
        scratch_shapes=scratch,
        compiler_params=pltpu.CompilerParams(vmem_limit_bytes=16 * 1024 * 1024),
        cost_estimate=pl.CostEstimate(flops=flops, bytes_accessed=moved, transcendentals=0),
    )(*ins)


def local(inputs, targets, row_order, mix_order, first_factor, up_factor, down_factor, last_factor):
    tokens = inputs.shape[0]
    count = tokens // N_HID
    steps = count // STEP
    piece_rows = BS * count // LANES
    loss_scale = 1.0 / math.sqrt(tokens)
    quarter_units = up_factor.shape[1]
    units = quarter_units * N_HID
    mix_row = mix_order[None, :]
    shape = jax.ShapeDtypeStruct
    pieces = shape((piece_rows, LANES), BF16)
    spread = pltpu.VMEM((piece_rows, LANES), F32)
    buffer = pltpu.VMEM((piece_rows, LANES), BF16)
    sems = pltpu.SemaphoreType.DMA((steps + 2,))
    flops = 2 * units * BS * count
    small = 2 * BS * BS * count

    (first_out,) = call(
        first_kernel,
        (inputs, first_factor),
        (pieces,),
        [pltpu.VMEM((count, BS), BF16), spread, buffer, sems],
        small,
        [HBM, VMEM],
        [HBM],
    )
    up_factor, down_factor, first_out = lax.optimization_barrier((up_factor, down_factor, first_out))
    arrived = exchange(first_out)

    up_far, down_far = from_partner(up_factor, 2), from_partner(down_factor, 2)
    ups = (up_factor, up_far, from_partner(up_factor, 1), from_partner(up_far, 1))
    downs = (down_factor, down_far, from_partner(down_factor, 1), from_partner(down_far, 1))
    rows = lax.dynamic_slice_in_dim(row_order, own_quarter() * count, count, 0)
    teacher = targets.at[rows].get(mode="promise_in_bounds")
    up_mixed, up_mixed_t, down, down_t, teacher_t, x_t = call(
        prepare_kernel,
        (inputs, teacher, mix_row) + ups + downs,
        (
            shape((units, BS), BF16),
            shape((BS, units), BF16),
            shape((units, BS), BF16),
            shape((BS, units), BF16),
            shape((BS, count), BF16),
            shape((BS, count), BF16),
        ),
        [pltpu.VMEM((count, BS), BF16), pltpu.SemaphoreType.DMA],
        2 * small,
        [HBM] + [VMEM] * 10,
    )

    summed, slope, hidden = call(
        forward_kernel,
        (arrived, up_mixed, down_t),
        (pieces, shape((units, count), F32), shape((units, count), BF16)),
        [pltpu.VMEM((units, count), BF16), spread, spread, sems],
        2 * flops,
        out_specs=[VMEM, VMEM, HBM],
    )
    returned = exchange(summed)

    grad_returned, err_grad = call(
        functools.partial(error_kernel, loss_scale),
        (returned, last_factor, teacher_t),
        (pieces, shape((BS, count), BF16)),
        [pltpu.VMEM((BS, count), BF16), spread, spread, sems],
        2 * small,
        out_specs=[VMEM, HBM],
    )
    grad_arrived = exchange(grad_returned)

    grad_grouped, grad_preact = call(
        backward_kernel,
        (grad_arrived, down, up_mixed_t, slope),
        (pieces, shape((units, count), BF16)),
        [pltpu.VMEM((units, count), BF16), spread, spread, buffer, sems],
        2 * flops,
        out_specs=[HBM, HBM],
    )
    grad_first_out = exchange(grad_grouped)

    half_rows = shape((units + BS, BS), F32)
    mine, theirs = call(
        weights_kernel,
        (arrived, returned, grad_arrived, hidden, grad_preact, err_grad),
        (half_rows, half_rows),
        [spread],
        2 * flops + small,
    )
    quarter_rows = shape((units // 2 + BS, BS), F32)
    mine, theirs = call(
        chip_sum_kernel, (mine, from_partner(theirs, 1)), (quarter_rows, quarter_rows), [], 0
    )
    factor_grad = shape((1, quarter_units, BS), F32)
    grad_up, grad_down, grad_last = call(
        totals_kernel,
        (mine, from_partner(theirs, 2), mix_row),
        (factor_grad, factor_grad, shape((1, BS, BS), F32)),
        [],
        0,
    )

    (grad_first,) = call(
        last_kernel, (grad_first_out, x_t), (shape((BS, BS), F32),), [spread], small
    )
    grad_first = sum_over_hid(grad_first)
    return (grad_first[None], grad_up, grad_down, grad_last)


def solution(mesh):
    placed = (
        P(None, "blk"),
        P(None, "blk"),
        P(),
        P(),
        P("blk", None, None),
        P("blk", "hid", None),
        P("blk", "hid", None),
        P("blk", None, None),
    )
    return jax.shard_map(
        local,
        mesh=mesh,
        in_specs=placed,
        out_specs=(
            P("blk", None, None),
            P("blk", "hid", None),
            P("blk", "hid", None),
            P("blk", None, None),
        ),
        check_vma=False,
    )
```

```python
import functools
import math

import jax
import jax.numpy as jnp
from jax import lax
from jax.experimental import pallas as pl
from jax.experimental.pallas import tpu as pltpu
from jax.sharding import PartitionSpec as P

BS = 128
NB = 64
N_HID = 4
LANES = 128
STEP = 256


def token_groups():
    return [
        [b * N_HID + (q ^ (2 * (b % 2))) for b in range(NB)] for q in range(N_HID)
    ]


def from_partner(value, m):
    return lax.ppermute(value, "hid", [(i, i ^ m) for i in range(N_HID)])


def exchange(rows):
    pieces = rows.reshape(NB, rows.shape[0] // NB, LANES)
    pieces = lax.all_to_all(
        pieces, ("blk", "hid"), 0, 0, tiled=True, axis_index_groups=token_groups()
    )
    return pieces.reshape(rows.shape)


def dot(a, b, dims):
    return lax.dot_general(a, b, (dims, ((), ())), preferred_element_type=jnp.float32)


def mm(a, b):
    return dot(a, b, ((1,), (0,)))


def sum_over_hid(part):
    got = [from_partner(part, m) for m in (1, 2, 3)]
    return (part + got[0]) + (got[1] + got[2])


def own_quarter():
    return lax.axis_index("hid") ^ (2 * (lax.axis_index("blk") % 2))


def put_pieces(spread, value, at):
    chunks = spread.shape[0] // BS
    for j in range(value.shape[1] // LANES):
        spread[pl.ds(at // LANES + j, BS, chunks), :] = value[:, j * LANES : (j + 1) * LANES]


def get_pieces(spread, at, size):
    chunks = spread.shape[0] // BS
    parts = [spread[pl.ds(at // LANES + j, BS, chunks), :] for j in range(size // LANES)]
    return jnp.concatenate(parts, axis=1).astype(jnp.bfloat16)


def send_out(spread, buffer, hbm, sems, first_sem):
    half = spread.shape[0] // 2
    copies = []
    for i in range(2):
        rows = pl.ds(i * half, half)
        buffer[rows, :] = spread[rows, :].astype(jnp.bfloat16)
        copies.append(pltpu.make_async_copy(buffer.at[rows], hbm.at[rows], sems.at[first_sem + i]))
        copies[-1].start()
    return copies


def first_kernel(
    x_hbm, first_hbm, up_hbm, down_hbm, order_hbm, out_hbm, packed_hbm, x_own_hbm, rows_hbm,
    x, first, spread, buffer, sems,
):
    count = x.shape[0]
    start = own_quarter() * count
    order_rows = rows_hbm.shape[0]
    steps = count // STEP
    units = up_hbm.shape[1]
    fetch_first = pltpu.make_async_copy(first_hbm, first, sems.at[steps])
    fetch_first.start()
    arrivals = []
    for i in range(steps):
        source = x_hbm.at[pl.ds(pl.multiple_of(start + i * STEP, STEP), STEP)]
        arrivals.append(pltpu.make_async_copy(source, x.at[pl.ds(i * STEP, STEP)], sems.at[i]))
        arrivals[-1].start()
    pack = [
        pltpu.make_async_copy(up_hbm.at[0], packed_hbm.at[pl.ds(0, units)], sems.at[steps + 1]),
        pltpu.make_async_copy(down_hbm.at[0], packed_hbm.at[pl.ds(units, units)], sems.at[steps + 2]),
        pltpu.make_async_copy(
            order_hbm.at[pl.ds(pl.multiple_of(own_quarter() * order_rows, order_rows), order_rows)],
            rows_hbm,
            sems.at[steps + 6],
        ),
    ]
    for copy in pack:
        copy.start()
    fetch_first.wait()
    first_t = first[0].T
    for i in range(steps):
        arrivals[i].wait()
        put_pieces(spread, dot(first_t, x[i * STEP : (i + 1) * STEP, :], ((1,), (1,))), i * STEP)
    copies = send_out(spread, buffer, out_hbm, sems, steps + 3)
    own = pltpu.make_async_copy(x, x_own_hbm, sems.at[steps + 5])
    own.start()
    for copy in pack + copies + [own]:
        copy.wait()


def unit_matrix():
    ids = lax.broadcasted_iota(jnp.int32, (BS, BS), 0)
    eye = (lax.broadcasted_iota(jnp.int32, (BS, BS), 1) == ids).astype(jnp.float32)
    return eye.astype(jnp.bfloat16)


def prepare_kernel(
    own_ref, far_ref, near_ref, other_ref, mix_ref, up_ref, down_t_ref, up_t_hbm, down_hbm, up_t, down, sems
):
    units = own_ref.shape[0] // 2
    refs = (own_ref, far_ref, near_ref, other_ref)
    ids = lax.broadcasted_iota(jnp.int32, (BS, BS), 0)
    one_hot = (mix_ref[...] == ids).astype(jnp.float32).astype(jnp.bfloat16)
    for i, ref in enumerate(refs):
        down[i * units : (i + 1) * units, :] = ref[units:, :]
    copies = [pltpu.make_async_copy(down, down_hbm, sems.at[0])]
    copies[0].start()
    up = jnp.concatenate([ref[0:units, :] for ref in refs])
    up_t[...] = dot(one_hot, up, ((1,), (1,))).astype(jnp.bfloat16)
    copies.append(pltpu.make_async_copy(up_t, up_t_hbm, sems.at[1]))
    copies[1].start()
    up_ref[...] = dot(up, one_hot, ((1,), (1,))).astype(jnp.bfloat16)
    down_t_ref[...] = dot(unit_matrix(), down[...], ((1,), (1,))).astype(jnp.bfloat16)
    for copy in copies:
        copy.wait()


def turn_kernel(in_ref, out_ref):
    out_ref[...] = dot(unit_matrix(), in_ref[...], ((1,), (1,))).astype(jnp.bfloat16)


def forward_kernel(
    in_ref, up_ref, down_t_ref, out_ref, slope_ref, hidden_ref, spread_in, spread
):
    spread_in[...] = in_ref[...].astype(jnp.float32)
    up = up_ref[...]
    down_t = down_t_ref[...]
    for at in range(0, hidden_ref.shape[1], STEP):
        preact = mm(up, get_pieces(spread_in, at, STEP))
        cdf = 0.5 * (1.0 + lax.erf(preact * (1.0 / math.sqrt(2.0))))
        dens = jnp.exp(-0.5 * preact * preact) * (1.0 / math.sqrt(2.0 * math.pi))
        hidden = (preact * cdf).astype(jnp.bfloat16)
        hidden_ref[:, at : at + STEP] = hidden
        slope_ref[:, at : at + STEP] = cdf + preact * dens
        put_pieces(spread, mm(down_t, hidden), at)
    out_ref[...] = spread[...].astype(jnp.bfloat16)


def error_kernel(scale, in_ref, last_ref, teacher_ref, out_ref, grad_ref, spread_in, spread):
    spread_in[...] = in_ref[...].astype(jnp.float32)
    last = last_ref[0]
    last_t = last.T
    grad_last = None
    for at in range(0, teacher_ref.shape[1], STEP):
        returned = get_pieces(spread_in, at, STEP)
        teacher = teacher_ref[:, at : at + STEP].astype(jnp.float32)
        err = ((mm(last_t, returned) - teacher) * scale).astype(jnp.bfloat16)
        put_pieces(spread, mm(last, err), at)
        part = dot(returned, err, ((1,), (1,)))
        grad_last = part if grad_last is None else grad_last + part
    out_ref[...] = spread[...].astype(jnp.bfloat16)
    grad_ref[...] = grad_last


def backward_kernel(
    in_ref, down_ref, up_t_ref, slope_ref, hidden_ref, out_hbm, grad_hbm, hidden_hbm,
    grad_ref, spread_in, spread, buffer, sems,
):
    copies = [pltpu.make_async_copy(hidden_ref, hidden_hbm, sems.at[2])]
    copies[0].start()
    spread_in[...] = in_ref[...].astype(jnp.float32)
    down = down_ref[...]
    up_t = up_t_ref[...]
    for i in range(grad_ref.shape[1] // STEP):
        columns = pl.ds(i * STEP, STEP)
        grad_hidden = mm(down, get_pieces(spread_in, i * STEP, STEP))
        grad = (grad_hidden * slope_ref[:, columns]).astype(jnp.bfloat16)
        grad_ref[:, columns] = grad
        copies.append(
            pltpu.make_async_copy(grad_ref.at[:, columns], grad_hbm.at[:, columns], sems.at[3 + i])
        )
        copies[-1].start()
        put_pieces(spread, mm(up_t, grad), i * STEP)
    for copy in send_out(spread, buffer, out_hbm, sems, 0) + copies:
        copy.wait()


def weights_kernel(
    arrived_hbm, grad_arrived_ref, hidden_hbm, grad_hbm, last_ref, mine_ref, theirs_ref,
    arrived, hidden, grad, spread_in, sems,
):
    units, count = hidden.shape
    half = units // 2
    copies = [
        pltpu.make_async_copy(hidden_hbm, hidden, sems.at[0]),
        pltpu.make_async_copy(arrived_hbm, arrived, sems.at[1]),
        pltpu.make_async_copy(grad_hbm, grad, sems.at[2]),
    ]
    for copy in copies:
        copy.start()

    def product(left):
        return dot(left[...], get_pieces(spread_in, 0, count), ((1,), (1,)))

    mine_ref[units:, :] = last_ref[...]
    theirs_ref[units:, :] = last_ref[...]
    spread_in[...] = grad_arrived_ref[...].astype(jnp.float32)
    copies[0].wait()
    down = product(hidden)
    mine_ref[half:units, :] = down[:half]
    theirs_ref[half:units, :] = down[half:]
    copies[1].wait()
    spread_in[...] = arrived[...].astype(jnp.float32)
    copies[2].wait()
    up = product(grad)
    mine_ref[0:half, :] = up[:half]
    theirs_ref[0:half, :] = up[half:]


def chip_sum_kernel(mine_ref, got_ref, mine_out, theirs_out):
    quarter = (mine_ref.shape[0] - BS) // 4
    total = mine_ref[...] + got_ref[...]
    mine_out[0:quarter, :] = total[0:quarter]
    theirs_out[0:quarter, :] = total[quarter : 2 * quarter]
    mine_out[quarter : 2 * quarter, :] = total[2 * quarter : 3 * quarter]
    theirs_out[quarter : 2 * quarter, :] = total[3 * quarter : 4 * quarter]
    mine_out[2 * quarter :, :] = total[4 * quarter :]
    theirs_out[2 * quarter :, :] = total[4 * quarter :]


def totals_kernel(mine_ref, got_ref, mix_ref, up_ref, down_ref, last_ref):
    quarter = up_ref.shape[1]
    total = mine_ref[...] + got_ref[...]
    ids = lax.broadcasted_iota(jnp.int32, (BS, BS), 0)
    one_hot = (mix_ref[...] == ids).astype(jnp.float32)
    up_ref[0] = jnp.dot(
        total[0:quarter], one_hot, precision=lax.Precision.HIGHEST, preferred_element_type=jnp.float32
    )
    down_ref[0] = total[quarter : 2 * quarter]
    last_ref[0] = total[2 * quarter :]


def last_kernel(in_ref, x_ref, out_ref, spread_in):
    spread_in[...] = in_ref[...].astype(jnp.float32)
    grad = get_pieces(spread_in, 0, x_ref.shape[0])
    out_ref[...] = mm(grad, x_ref[...]).T


VMEM = pl.BlockSpec(memory_space=pltpu.VMEM)
HBM = pl.BlockSpec(memory_space=pltpu.HBM)
BF16 = jnp.bfloat16
F32 = jnp.float32


def call(kernel, ins, outs, scratch, flops, in_specs=None, out_specs=None, pin=True):
    moved = sum(a.size * a.dtype.itemsize for a in ins) + sum(
        math.prod(o.shape) * o.dtype.itemsize for o in outs
    )
    if in_specs:
        ins = [
            pltpu.with_memory_space_constraint(a, pltpu.HBM) if spec is HBM else a
            for a, spec in zip(ins, in_specs)
        ]
    places = out_specs or [VMEM] * len(outs)
    if pin:
        outs = tuple(
            (pltpu.HBM if spec is HBM else pltpu.VMEM)(o.shape, o.dtype) for o, spec in zip(outs, places)
        )
    return pl.pallas_call(
        kernel,
        out_shape=outs,
        in_specs=in_specs or [VMEM] * len(ins),
        out_specs=out_specs or [VMEM] * len(outs),
        scratch_shapes=scratch,
        compiler_params=pltpu.CompilerParams(vmem_limit_bytes=16 * 1024 * 1024),
        cost_estimate=pl.CostEstimate(flops=flops, bytes_accessed=moved, transcendentals=0),
    )(*ins)


def local(inputs, targets, row_order, mix_order, first_factor, up_factor, down_factor, last_factor):
    tokens = inputs.shape[0]
    count = tokens // N_HID
    steps = count // STEP
    piece_rows = BS * count // LANES
    loss_scale = 1.0 / math.sqrt(tokens)
    quarter_units = up_factor.shape[1]
    units = quarter_units * N_HID
    mix_row = mix_order[None, :]
    shape = jax.ShapeDtypeStruct
    pieces = shape((piece_rows, LANES), BF16)
    spread = pltpu.VMEM((piece_rows, LANES), F32)
    buffer = pltpu.VMEM((piece_rows, LANES), BF16)
    flops = 2 * units * BS * count
    small = 2 * BS * BS * count
    two_sems = pltpu.SemaphoreType.DMA((2,))

    first_out, weights, x_own, rows = call(
        first_kernel,
        (inputs, first_factor, up_factor, down_factor, row_order.reshape(-1, LANES)),
        (
            pieces,
            shape((2 * quarter_units, BS), BF16),
            shape((count, BS), BF16),
            shape((count // LANES, LANES), jnp.int32),
        ),
        [
            pltpu.VMEM((count, BS), BF16),
            pltpu.VMEM((1, BS, BS), BF16),
            spread,
            buffer,
            pltpu.SemaphoreType.DMA((steps + 7,)),
        ],
        small,
        [HBM] * 5,
        [HBM] * 4,
    )
    far = from_partner(weights, 2)
    arrived = exchange(first_out)

    teacher = targets.at[rows.reshape(count)].get(mode="promise_in_bounds")
    (teacher_t,) = call(turn_kernel, (teacher,), (shape((BS, count), BF16),), [], small)
    up_mixed, down_t, up_mixed_t, down = call(
        prepare_kernel,
        (weights, far, from_partner(weights, 1), from_partner(weights, 3), mix_row),
        (
            shape((units, BS), BF16),
            shape((BS, units), BF16),
            shape((BS, units), BF16),
            shape((units, BS), BF16),
        ),
        [pltpu.VMEM((BS, units), BF16), pltpu.VMEM((units, BS), BF16), two_sems],
        small,
        out_specs=[VMEM, VMEM, HBM, HBM],
    )
    teacher_t, arrived = lax.optimization_barrier((teacher_t, arrived))

    summed, slope, hidden = call(
        forward_kernel,
        (arrived, up_mixed, down_t),
        (pieces, shape((units, count), F32), shape((units, count), BF16)),
        [spread, spread],
        2 * flops,
    )
    returned = exchange(summed)

    grad_returned, grad_last = call(
        functools.partial(error_kernel, loss_scale),
        (returned, last_factor, teacher_t),
        (pieces, shape((BS, BS), F32)),
        [spread, spread],
        3 * small,
    )
    grad_arrived = exchange(grad_returned)

    grad_grouped, grad_preact, hidden = call(
        backward_kernel,
        (grad_arrived, down, up_mixed_t, slope, hidden),
        (pieces, shape((units, count), BF16), shape((units, count), BF16)),
        [
            pltpu.VMEM((units, count), BF16),
            spread,
            spread,
            buffer,
            pltpu.SemaphoreType.DMA((steps + 3,)),
        ],
        2 * flops,
        out_specs=[HBM, HBM, HBM],
    )
    grad_first_out = exchange(grad_grouped)

    half_rows = shape((units + BS, BS), F32)
    mine, theirs = call(
        weights_kernel,
        (arrived, grad_arrived, hidden, grad_preact, grad_last),
        (half_rows, half_rows),
        [
            buffer,
            pltpu.VMEM((units, count), BF16),
            pltpu.VMEM((units, count), BF16),
            spread,
            pltpu.SemaphoreType.DMA((3,)),
        ],
        2 * flops,
        [HBM, VMEM, HBM, HBM, VMEM],
    )
    quarter_rows = shape((units // 2 + BS, BS), F32)
    mine, theirs = call(
        chip_sum_kernel, (mine, from_partner(theirs, 1)), (quarter_rows, quarter_rows), [], 0
    )
    factor_grad = shape((1, quarter_units, BS), F32)
    grad_up, grad_down, grad_last = call(
        totals_kernel,
        (mine, from_partner(theirs, 2), mix_row),
        (factor_grad, factor_grad, shape((1, BS, BS), F32)),
        [],
        0,
        pin=False,
    )

    (grad_first,) = call(
        last_kernel, (grad_first_out, x_own), (shape((BS, BS), F32),), [spread], small
    )
    grad_first = sum_over_hid(grad_first)
    return (grad_first[None], grad_up, grad_down, grad_last)


def solution(mesh):
    placed = (
        P(None, "blk"),
        P(None, "blk"),
        P(),
        P(),
        P("blk", None, None),
        P("blk", "hid", None),
        P("blk", "hid", None),
        P("blk", None, None),
    )
    return jax.shard_map(
        local,
        mesh=mesh,
        in_specs=placed,
        out_specs=(
            P("blk", None, None),
            P("blk", "hid", None),
            P("blk", "hid", None),
            P("blk", None, None),
        ),
        check_vma=False,
    )
```

```python
import functools
import math

import jax
import jax.numpy as jnp
from jax import lax
from jax.experimental import pallas as pl
from jax.experimental.pallas import tpu as pltpu
from jax.sharding import PartitionSpec as P

BS = 128
NB = 64
N_HID = 4
LANES = 128
STEP = 1024


def token_groups():
    return [
        [b * N_HID + (q ^ (2 * (b % 2))) for b in range(NB)] for q in range(N_HID)
    ]


def from_partner(value, m):
    return lax.ppermute(value, "hid", [(i, i ^ m) for i in range(N_HID)])


def exchange(rows):
    pieces = rows.reshape(NB, rows.shape[0] // NB, LANES)
    pieces = lax.all_to_all(
        pieces, ("blk", "hid"), 0, 0, tiled=True, axis_index_groups=token_groups()
    )
    return pieces.reshape(rows.shape)


def dot(a, b, dims):
    return lax.dot_general(a, b, (dims, ((), ())), preferred_element_type=jnp.float32)


def mm(a, b):
    return dot(a, b, ((1,), (0,)))


def sum_over_hid(part):
    got = [from_partner(part, m).astype(jnp.float32) for m in (1, 2, 3)]
    return (part.astype(jnp.float32) + got[0]) + (got[1] + got[2])


def own_quarter():
    return lax.axis_index("hid") ^ (2 * (lax.axis_index("blk") % 2))


def put_pieces(spread, value, at):
    chunks = spread.shape[0] // BS
    for j in range(value.shape[1] // LANES):
        spread[pl.ds(at // LANES + j, BS, chunks), :] = value[:, j * LANES : (j + 1) * LANES]


def get_pieces(spread, at, size):
    chunks = spread.shape[0] // BS
    parts = [spread[pl.ds(at // LANES + j, BS, chunks), :] for j in range(size // LANES)]
    return jnp.concatenate(parts, axis=1).astype(jnp.bfloat16)


def send_out(spread, buffer, hbm, sems, first_sem):
    half = spread.shape[0] // 2
    copies = []
    for i in range(2):
        rows = pl.ds(i * half, half)
        buffer[rows, :] = spread[rows, :].astype(jnp.bfloat16)
        copies.append(pltpu.make_async_copy(buffer.at[rows], hbm.at[rows], sems.at[first_sem + i]))
        copies[-1].start()
    return copies


def first_kernel(
    x_hbm, first_hbm, up_hbm, down_hbm, order_hbm, out_hbm, packed_hbm, x_own_hbm, rows_hbm,
    x, first, spread, buffer, sems,
):
    count = x.shape[0]
    start = own_quarter() * count
    order_rows = rows_hbm.shape[0]
    steps = count // STEP
    units = up_hbm.shape[1]
    fetch_first = pltpu.make_async_copy(first_hbm, first, sems.at[steps])
    fetch_first.start()
    arrivals = []
    for i in range(steps):
        source = x_hbm.at[pl.ds(pl.multiple_of(start + i * STEP, STEP), STEP)]
        arrivals.append(pltpu.make_async_copy(source, x.at[pl.ds(i * STEP, STEP)], sems.at[i]))
        arrivals[-1].start()
    pack = [
        pltpu.make_async_copy(up_hbm.at[0], packed_hbm.at[pl.ds(0, units)], sems.at[steps + 1]),
        pltpu.make_async_copy(down_hbm.at[0], packed_hbm.at[pl.ds(units, units)], sems.at[steps + 2]),
        pltpu.make_async_copy(
            order_hbm.at[pl.ds(pl.multiple_of(own_quarter() * order_rows, order_rows), order_rows)],
            rows_hbm,
            sems.at[steps + 6],
        ),
    ]
    for copy in pack:
        copy.start()
    fetch_first.wait()
    first_t = first[0].T
    for arrival in arrivals:
        arrival.wait()
    own = pltpu.make_async_copy(x, x_own_hbm, sems.at[steps + 5])
    own.start()
    put_pieces(spread, dot(first_t, x[...], ((1,), (1,))), 0)
    copies = send_out(spread, buffer, out_hbm, sems, steps + 3)
    for copy in pack + copies + [own]:
        copy.wait()


def unit_matrix():
    ids = lax.broadcasted_iota(jnp.int32, (BS, BS), 0)
    eye = (lax.broadcasted_iota(jnp.int32, (BS, BS), 1) == ids).astype(jnp.float32)
    return eye.astype(jnp.bfloat16)


def prepare_kernel(
    own_ref, far_ref, near_ref, other_ref, mix_ref, up_ref, down_t_ref, up_t_hbm, down_hbm, up_t, down, sems
):
    units = own_ref.shape[0] // 2
    refs = (own_ref, far_ref, near_ref, other_ref)
    ids = lax.broadcasted_iota(jnp.int32, (BS, BS), 0)
    one_hot = (mix_ref[...] == ids).astype(jnp.float32).astype(jnp.bfloat16)
    for i, ref in enumerate(refs):
        down[i * units : (i + 1) * units, :] = ref[units:, :]
    copies = [pltpu.make_async_copy(down, down_hbm, sems.at[0])]
    copies[0].start()
    up = jnp.concatenate([ref[0:units, :] for ref in refs])
    up_t[...] = dot(one_hot, up, ((1,), (1,))).astype(jnp.bfloat16)
    copies.append(pltpu.make_async_copy(up_t, up_t_hbm, sems.at[1]))
    copies[1].start()
    up_ref[...] = dot(up, one_hot, ((1,), (1,))).astype(jnp.bfloat16)
    down_t_ref[...] = dot(unit_matrix(), down[...], ((1,), (1,))).astype(jnp.bfloat16)
    for copy in copies:
        copy.wait()


def turn_kernel(in_ref, out_ref):
    out_ref[...] = dot(unit_matrix(), in_ref[...], ((1,), (1,))).astype(jnp.bfloat16)


def forward_kernel(
    in_ref, up_ref, down_t_ref, out_ref, slope_ref, hidden_ref, spread_in, spread
):
    spread_in[...] = in_ref[...].astype(jnp.float32)
    up = up_ref[...]
    down_t = down_t_ref[...]
    for at in range(0, hidden_ref.shape[1], STEP):
        preact = mm(up, get_pieces(spread_in, at, STEP))
        cdf = 0.5 * (1.0 + lax.erf(preact * (1.0 / math.sqrt(2.0))))
        dens = jnp.exp(-0.5 * preact * preact) * (1.0 / math.sqrt(2.0 * math.pi))
        hidden = (preact * cdf).astype(jnp.bfloat16)
        hidden_ref[:, at : at + STEP] = hidden
        slope_ref[:, at : at + STEP] = cdf + preact * dens
        put_pieces(spread, mm(down_t, hidden), at)
    out_ref[...] = spread[...].astype(jnp.bfloat16)


def error_kernel(scale, in_ref, last_ref, teacher_ref, out_ref, grad_ref, spread_in, spread):
    spread_in[...] = in_ref[...].astype(jnp.float32)
    last = last_ref[0]
    last_t = last.T
    grad_last = None
    for at in range(0, teacher_ref.shape[1], STEP):
        returned = get_pieces(spread_in, at, STEP)
        teacher = teacher_ref[:, at : at + STEP].astype(jnp.float32)
        err = ((mm(last_t, returned) - teacher) * scale).astype(jnp.bfloat16)
        put_pieces(spread, mm(last, err), at)
        part = dot(returned, err, ((1,), (1,)))
        grad_last = part if grad_last is None else grad_last + part
    out_ref[...] = spread[...].astype(jnp.bfloat16)
    grad_ref[...] = grad_last


def backward_kernel(
    in_ref, down_ref, up_t_ref, slope_ref, hidden_ref, out_hbm, grad_hbm, hidden_hbm,
    grad_ref, spread_in, spread, buffer, sems,
):
    copies = [pltpu.make_async_copy(hidden_ref, hidden_hbm, sems.at[2])]
    copies[0].start()
    spread_in[...] = in_ref[...].astype(jnp.float32)
    down = down_ref[...]
    up_t = up_t_ref[...]
    for i in range(grad_ref.shape[1] // STEP):
        columns = pl.ds(i * STEP, STEP)
        grad_hidden = mm(down, get_pieces(spread_in, i * STEP, STEP))
        grad = (grad_hidden * slope_ref[:, columns]).astype(jnp.bfloat16)
        grad_ref[:, columns] = grad
        copies.append(
            pltpu.make_async_copy(grad_ref.at[:, columns], grad_hbm.at[:, columns], sems.at[3 + i])
        )
        copies[-1].start()
        put_pieces(spread, mm(up_t, grad), i * STEP)
    for copy in send_out(spread, buffer, out_hbm, sems, 0) + copies:
        copy.wait()


def weights_kernel(
    arrived_hbm, grad_arrived_ref, hidden_hbm, grad_hbm, last_ref, mine_ref, theirs_ref,
    arrived, hidden, grad, spread_in, sems,
):
    units, count = hidden.shape
    half = units // 2
    copies = [
        pltpu.make_async_copy(hidden_hbm, hidden, sems.at[0]),
        pltpu.make_async_copy(arrived_hbm, arrived, sems.at[1]),
        pltpu.make_async_copy(grad_hbm, grad, sems.at[2]),
    ]
    for copy in copies:
        copy.start()

    def product(left):
        return dot(left[...], get_pieces(spread_in, 0, count), ((1,), (1,)))

    mine_ref[units:, :] = last_ref[...]
    theirs_ref[units:, :] = last_ref[...]
    spread_in[...] = grad_arrived_ref[...].astype(jnp.float32)
    copies[0].wait()
    down = product(hidden)
    mine_ref[half:units, :] = down[:half]
    theirs_ref[half:units, :] = down[half:]
    copies[1].wait()
    spread_in[...] = arrived[...].astype(jnp.float32)
    copies[2].wait()
    up = product(grad)
    mine_ref[0:half, :] = up[:half]
    theirs_ref[0:half, :] = up[half:]


def chip_sum_kernel(mine_ref, got_ref, mine_out, theirs_out):
    quarter = (mine_ref.shape[0] - BS) // 4
    total = mine_ref[...] + got_ref[...]
    mine_out[0:quarter, :] = total[0:quarter]
    theirs_out[0:quarter, :] = total[quarter : 2 * quarter]
    mine_out[quarter : 2 * quarter, :] = total[2 * quarter : 3 * quarter]
    theirs_out[quarter : 2 * quarter, :] = total[3 * quarter : 4 * quarter]
    mine_out[2 * quarter :, :] = total[4 * quarter :]
    theirs_out[2 * quarter :, :] = total[4 * quarter :]


def totals_kernel(mine_ref, got_ref, mix_ref, up_ref, down_ref, last_ref):
    quarter = up_ref.shape[1]
    total = mine_ref[...] + got_ref[...]
    ids = lax.broadcasted_iota(jnp.int32, (BS, BS), 0)
    one_hot = (mix_ref[...] == ids).astype(jnp.float32)
    up_ref[0] = jnp.dot(
        total[0:quarter], one_hot, precision=lax.Precision.HIGHEST, preferred_element_type=jnp.float32
    )
    down_ref[0] = total[quarter : 2 * quarter]
    last_ref[0] = total[2 * quarter :]


def last_kernel(in_ref, x_ref, out_ref, spread_in):
    spread_in[...] = in_ref[...].astype(jnp.float32)
    grad = get_pieces(spread_in, 0, x_ref.shape[0])
    out_ref[...] = mm(grad, x_ref[...]).T.astype(jnp.bfloat16)


VMEM = pl.BlockSpec(memory_space=pltpu.VMEM)
HBM = pl.BlockSpec(memory_space=pltpu.HBM)
BF16 = jnp.bfloat16
F32 = jnp.float32


def call(kernel, ins, outs, scratch, flops, in_specs=None, out_specs=None, pin=True):
    moved = sum(a.size * a.dtype.itemsize for a in ins) + sum(
        math.prod(o.shape) * o.dtype.itemsize for o in outs
    )
    if in_specs:
        ins = [
            pltpu.with_memory_space_constraint(a, pltpu.HBM) if spec is HBM else a
            for a, spec in zip(ins, in_specs)
        ]
    places = out_specs or [VMEM] * len(outs)
    if pin:
        outs = tuple(
            (pltpu.HBM if spec is HBM else pltpu.VMEM)(o.shape, o.dtype) for o, spec in zip(outs, places)
        )
    return pl.pallas_call(
        kernel,
        out_shape=outs,
        in_specs=in_specs or [VMEM] * len(ins),
        out_specs=out_specs or [VMEM] * len(outs),
        scratch_shapes=scratch,
        compiler_params=pltpu.CompilerParams(vmem_limit_bytes=16 * 1024 * 1024),
        cost_estimate=pl.CostEstimate(flops=flops, bytes_accessed=moved, transcendentals=0),
    )(*ins)


def local(inputs, targets, row_order, mix_order, first_factor, up_factor, down_factor, last_factor):
    tokens = inputs.shape[0]
    count = tokens // N_HID
    steps = count // STEP
    piece_rows = BS * count // LANES
    loss_scale = 1.0 / math.sqrt(tokens)
    quarter_units = up_factor.shape[1]
    units = quarter_units * N_HID
    mix_row = mix_order[None, :]
    shape = jax.ShapeDtypeStruct
    pieces = shape((piece_rows, LANES), BF16)
    spread = pltpu.VMEM((piece_rows, LANES), F32)
    buffer = pltpu.VMEM((piece_rows, LANES), BF16)
    flops = 2 * units * BS * count
    small = 2 * BS * BS * count
    two_sems = pltpu.SemaphoreType.DMA((2,))

    first_out, weights, x_own, rows = call(
        first_kernel,
        (inputs, first_factor, up_factor, down_factor, row_order.reshape(-1, LANES)),
        (
            pieces,
            shape((2 * quarter_units, BS), BF16),
            shape((count, BS), BF16),
            shape((count // LANES, LANES), jnp.int32),
        ),
        [
            pltpu.VMEM((count, BS), BF16),
            pltpu.VMEM((1, BS, BS), BF16),
            spread,
            buffer,
            pltpu.SemaphoreType.DMA((steps + 7,)),
        ],
        small,
        [HBM] * 5,
        [HBM] * 4,
    )
    far = from_partner(weights, 2)
    arrived = exchange(first_out)

    teacher = targets.at[rows.reshape(count)].get(mode="promise_in_bounds", wrap_negative_indices=False)
    weights, far, teacher = lax.optimization_barrier((weights, far, teacher))
    near, other = from_partner(weights, 1), from_partner(far, 1)
    (teacher_t,) = call(turn_kernel, (teacher,), (shape((BS, count), BF16),), [], small)
    up_mixed, down_t, up_mixed_t, down = call(
        prepare_kernel,
        (weights, far, near, other, mix_row),
        (
            shape((units, BS), BF16),
            shape((BS, units), BF16),
            shape((BS, units), BF16),
            shape((units, BS), BF16),
        ),
        [pltpu.VMEM((BS, units), BF16), pltpu.VMEM((units, BS), BF16), two_sems],
        small,
        out_specs=[VMEM, VMEM, HBM, HBM],
    )
    teacher_t, arrived = lax.optimization_barrier((teacher_t, arrived))

    summed, slope, hidden = call(
        forward_kernel,
        (arrived, up_mixed, down_t),
        (pieces, shape((units, count), F32), shape((units, count), BF16)),
        [spread, spread],
        2 * flops,
    )
    returned = exchange(summed)

    grad_returned, grad_last = call(
        functools.partial(error_kernel, loss_scale),
        (returned, last_factor, teacher_t),
        (pieces, shape((BS, BS), F32)),
        [spread, spread],
        3 * small,
    )
    grad_arrived = exchange(grad_returned)

    grad_grouped, grad_preact, hidden = call(
        backward_kernel,
        (grad_arrived, down, up_mixed_t, slope, hidden),
        (pieces, shape((units, count), BF16), shape((units, count), BF16)),
        [
            pltpu.VMEM((units, count), BF16),
            spread,
            spread,
            buffer,
            pltpu.SemaphoreType.DMA((steps + 3,)),
        ],
        2 * flops,
        out_specs=[HBM, HBM, HBM],
    )
    grad_first_out = exchange(grad_grouped)

    half_rows = shape((units + BS, BS), F32)
    mine, theirs = call(
        weights_kernel,
        (arrived, grad_arrived, hidden, grad_preact, grad_last),
        (half_rows, half_rows),
        [
            buffer,
            pltpu.VMEM((units, count), BF16),
            pltpu.VMEM((units, count), BF16),
            spread,
            pltpu.SemaphoreType.DMA((3,)),
        ],
        2 * flops,
        [HBM, VMEM, HBM, HBM, VMEM],
    )
    quarter_rows = shape((units // 2 + BS, BS), F32)
    mine, theirs = call(
        chip_sum_kernel, (mine, from_partner(theirs, 1)), (quarter_rows, quarter_rows), [], 0
    )
    factor_grad = shape((1, quarter_units, BS), F32)
    grad_up, grad_down, grad_last = call(
        totals_kernel,
        (mine, from_partner(theirs, 2), mix_row),
        (factor_grad, factor_grad, shape((1, BS, BS), F32)),
        [],
        0,
        pin=False,
    )

    (grad_first,) = call(
        last_kernel, (grad_first_out, x_own), (shape((BS, BS), BF16),), [spread], small
    )
    grad_first = sum_over_hid(grad_first)
    return (grad_first[None], grad_up, grad_down, grad_last)


def solution(mesh):
    placed = (
        P(None, "blk"),
        P(None, "blk"),
        P(),
        P(),
        P("blk", None, None),
        P("blk", "hid", None),
        P("blk", "hid", None),
        P("blk", None, None),
    )
    return jax.shard_map(
        local,
        mesh=mesh,
        in_specs=placed,
        out_specs=(
            P("blk", None, None),
            P("blk", "hid", None),
            P("blk", "hid", None),
            P("blk", None, None),
        ),
        check_vma=False,
    )
```

```python
import functools
import math

import jax
import jax.numpy as jnp
from jax import lax
from jax.experimental import pallas as pl
from jax.experimental.pallas import tpu as pltpu
from jax.sharding import PartitionSpec as P

BS = 128
NB = 64
N_HID = 4
LANES = 128
STEP = 1024


def token_groups():
    return [
        [b * N_HID + (q ^ (2 * (b % 2))) for b in range(NB)] for q in range(N_HID)
    ]


def from_partner(value, m):
    return lax.ppermute(value, "hid", [(i, i ^ m) for i in range(N_HID)])


def exchange(rows):
    pieces = rows.reshape(NB, rows.shape[0] // NB, LANES)
    pieces = lax.all_to_all(
        pieces, ("blk", "hid"), 0, 0, tiled=True, axis_index_groups=token_groups()
    )
    return pieces.reshape(rows.shape)


def dot(a, b, dims):
    return lax.dot_general(a, b, (dims, ((), ())), preferred_element_type=jnp.float32)


def mm(a, b):
    return dot(a, b, ((1,), (0,)))


def sum_over_hid(part):
    got = [from_partner(part, m).astype(jnp.float32) for m in (1, 2, 3)]
    return (part.astype(jnp.float32) + got[0]) + (got[1] + got[2])


def own_quarter():
    return lax.axis_index("hid") ^ (2 * (lax.axis_index("blk") % 2))


def put_pieces(spread, value, at):
    chunks = spread.shape[0] // BS
    for j in range(value.shape[1] // LANES):
        spread[pl.ds(at // LANES + j, BS, chunks), :] = value[:, j * LANES : (j + 1) * LANES]


def get_pieces(spread, at, size):
    chunks = spread.shape[0] // BS
    parts = [spread[pl.ds(at // LANES + j, BS, chunks), :] for j in range(size // LANES)]
    return jnp.concatenate(parts, axis=1).astype(jnp.bfloat16)


def send_out(spread, buffer, hbm, sems, first_sem):
    half = spread.shape[0] // 2
    copies = []
    for i in range(2):
        rows = pl.ds(i * half, half)
        buffer[rows, :] = spread[rows, :].astype(jnp.bfloat16)
        copies.append(pltpu.make_async_copy(buffer.at[rows], hbm.at[rows], sems.at[first_sem + i]))
        copies[-1].start()
    return copies


def first_kernel(
    x_hbm, first_hbm, up_hbm, down_hbm, order_hbm, out_hbm, packed_hbm, x_own_hbm, rows_hbm,
    x, first, packed, rows, spread, buffer, sems,
):
    count = x.shape[0]
    units = up_hbm.shape[1]
    order_rows = rows.shape[0]
    start = pl.multiple_of(own_quarter() * count, count)
    order_start = pl.multiple_of(own_quarter() * order_rows, order_rows)
    fetch = [
        (x_hbm.at[pl.ds(start, count)], x),
        (first_hbm, first),
        (up_hbm.at[0], packed.at[pl.ds(0, units)]),
        (down_hbm.at[0], packed.at[pl.ds(units, units)]),
        (order_hbm.at[pl.ds(order_start, order_rows)], rows),
    ]
    fetch = [pltpu.make_async_copy(a, b, sems.at[i]) for i, (a, b) in enumerate(fetch)]
    for copy in fetch:
        copy.start()
    fetch[1].wait()
    first_t = first[0].T
    fetch[0].wait()
    put_pieces(spread, dot(first_t, x[...], ((1,), (1,))), 0)
    copies = send_out(spread, buffer, out_hbm, sems, 5)
    for copy in fetch[2:]:
        copy.wait()
    for i, (source, target) in enumerate(((x, x_own_hbm), (packed, packed_hbm), (rows, rows_hbm))):
        copies.append(pltpu.make_async_copy(source, target, sems.at[7 + i]))
        copies[-1].start()
    for copy in copies:
        copy.wait()


def unit_matrix():
    ids = lax.broadcasted_iota(jnp.int32, (BS, BS), 0)
    eye = (lax.broadcasted_iota(jnp.int32, (BS, BS), 1) == ids).astype(jnp.float32)
    return eye.astype(jnp.bfloat16)


def prepare_kernel(
    own_ref, far_ref, near_ref, other_ref, mix_ref, up_ref, down_t_ref, up_t_hbm, down_hbm, up_t, down, sems
):
    units = own_ref.shape[0] // 2
    refs = (own_ref, far_ref, near_ref, other_ref)
    ids = lax.broadcasted_iota(jnp.int32, (BS, BS), 0)
    one_hot = (mix_ref[...] == ids).astype(jnp.float32).astype(jnp.bfloat16)
    for i, ref in enumerate(refs):
        down[i * units : (i + 1) * units, :] = ref[units:, :]
    copies = [pltpu.make_async_copy(down, down_hbm, sems.at[0])]
    copies[0].start()
    up = jnp.concatenate([ref[0:units, :] for ref in refs])
    up_t[...] = dot(one_hot, up, ((1,), (1,))).astype(jnp.bfloat16)
    copies.append(pltpu.make_async_copy(up_t, up_t_hbm, sems.at[1]))
    copies[1].start()
    up_ref[...] = dot(up, one_hot, ((1,), (1,))).astype(jnp.bfloat16)
    down_t_ref[...] = dot(unit_matrix(), down[...], ((1,), (1,))).astype(jnp.bfloat16)
    for copy in copies:
        copy.wait()


def turn_kernel(in_ref, out_ref):
    out_ref[...] = dot(unit_matrix(), in_ref[...], ((1,), (1,))).astype(jnp.bfloat16)


def forward_kernel(
    in_ref, up_ref, down_t_ref, out_ref, slope_ref, hidden_ref, spread_in, spread
):
    spread_in[...] = in_ref[...].astype(jnp.float32)
    up = up_ref[...]
    down_t = down_t_ref[...]
    for at in range(0, hidden_ref.shape[1], STEP):
        preact = mm(up, get_pieces(spread_in, at, STEP))
        cdf = 0.5 * (1.0 + lax.erf(preact * (1.0 / math.sqrt(2.0))))
        dens = jnp.exp(-0.5 * preact * preact) * (1.0 / math.sqrt(2.0 * math.pi))
        hidden = (preact * cdf).astype(jnp.bfloat16)
        hidden_ref[:, at : at + STEP] = hidden
        slope_ref[:, at : at + STEP] = cdf + preact * dens
        put_pieces(spread, mm(down_t, hidden), at)
    out_ref[...] = spread[...].astype(jnp.bfloat16)


def error_kernel(scale, in_ref, last_ref, teacher_ref, out_ref, grad_ref, spread_in, spread):
    spread_in[...] = in_ref[...].astype(jnp.float32)
    last = last_ref[0]
    last_t = last.T
    grad_last = None
    for at in range(0, teacher_ref.shape[1], STEP):
        returned = get_pieces(spread_in, at, STEP)
        teacher = teacher_ref[:, at : at + STEP].astype(jnp.float32)
        err = ((mm(last_t, returned) - teacher) * scale).astype(jnp.bfloat16)
        put_pieces(spread, mm(last, err), at)
        part = dot(returned, err, ((1,), (1,)))
        grad_last = part if grad_last is None else grad_last + part
    out_ref[...] = spread[...].astype(jnp.bfloat16)
    grad_ref[...] = grad_last


def backward_kernel(
    in_ref, down_ref, up_t_ref, slope_ref, hidden_ref, arrived_ref, last_ref,
    out_hbm, mine_ref, theirs_ref, spread_in, spread, buffer, sems,
):
    units, count = hidden_ref.shape
    half = units // 2
    spread_in[...] = in_ref[...].astype(jnp.float32)
    grad_out = get_pieces(spread_in, 0, count)
    grad_hidden = mm(down_ref[...], grad_out)
    grad = (grad_hidden * slope_ref[...]).astype(jnp.bfloat16)
    put_pieces(spread, mm(up_t_ref[...], grad), 0)
    copies = send_out(spread, buffer, out_hbm, sems, 0)
    mine_ref[units:, :] = last_ref[...]
    theirs_ref[units:, :] = last_ref[...]
    down = dot(hidden_ref[...], grad_out, ((1,), (1,)))
    mine_ref[half:units, :] = down[:half]
    theirs_ref[half:units, :] = down[half:]
    spread_in[...] = arrived_ref[...].astype(jnp.float32)
    up = dot(grad, get_pieces(spread_in, 0, count), ((1,), (1,)))
    mine_ref[0:half, :] = up[:half]
    theirs_ref[0:half, :] = up[half:]
    for copy in copies:
        copy.wait()


def chip_sum_kernel(mine_ref, got_ref, mine_out, theirs_out):
    quarter = (mine_ref.shape[0] - BS) // 4
    total = mine_ref[...] + got_ref[...]
    mine_out[0:quarter, :] = total[0:quarter]
    theirs_out[0:quarter, :] = total[quarter : 2 * quarter]
    mine_out[quarter : 2 * quarter, :] = total[2 * quarter : 3 * quarter]
    theirs_out[quarter : 2 * quarter, :] = total[3 * quarter : 4 * quarter]
    mine_out[2 * quarter :, :] = total[4 * quarter :]
    theirs_out[2 * quarter :, :] = total[4 * quarter :]


def totals_kernel(mine_ref, got_ref, mix_ref, up_ref, down_ref, last_ref):
    quarter = up_ref.shape[1]
    total = mine_ref[...] + got_ref[...]
    ids = lax.broadcasted_iota(jnp.int32, (BS, BS), 0)
    one_hot = (mix_ref[...] == ids).astype(jnp.float32)
    up_ref[0] = jnp.dot(
        total[0:quarter], one_hot, precision=lax.Precision.HIGHEST, preferred_element_type=jnp.float32
    )
    down_ref[0] = total[quarter : 2 * quarter]
    last_ref[0] = total[2 * quarter :]


def last_kernel(in_ref, x_ref, out_ref, spread_in):
    spread_in[...] = in_ref[...].astype(jnp.float32)
    grad = get_pieces(spread_in, 0, x_ref.shape[0])
    out_ref[...] = mm(grad, x_ref[...]).T.astype(jnp.bfloat16)


VMEM = pl.BlockSpec(memory_space=pltpu.VMEM)
HBM = pl.BlockSpec(memory_space=pltpu.HBM)
BF16 = jnp.bfloat16
F32 = jnp.float32


def call(kernel, ins, outs, scratch, flops, in_specs=None, out_specs=None, pin=True):
    moved = sum(a.size * a.dtype.itemsize for a in ins) + sum(
        math.prod(o.shape) * o.dtype.itemsize for o in outs
    )
    if in_specs:
        ins = [
            pltpu.with_memory_space_constraint(a, pltpu.HBM) if spec is HBM else a
            for a, spec in zip(ins, in_specs)
        ]
    places = out_specs or [VMEM] * len(outs)
    if pin:
        outs = tuple(
            (pltpu.HBM if spec is HBM else pltpu.VMEM)(o.shape, o.dtype) for o, spec in zip(outs, places)
        )
    return pl.pallas_call(
        kernel,
        out_shape=outs,
        in_specs=in_specs or [VMEM] * len(ins),
        out_specs=out_specs or [VMEM] * len(outs),
        scratch_shapes=scratch,
        compiler_params=pltpu.CompilerParams(vmem_limit_bytes=16 * 1024 * 1024),
        cost_estimate=pl.CostEstimate(flops=flops, bytes_accessed=moved, transcendentals=0),
    )(*ins)


def local(inputs, targets, row_order, mix_order, first_factor, up_factor, down_factor, last_factor):
    tokens = inputs.shape[0]
    count = tokens // N_HID
    steps = count // STEP
    piece_rows = BS * count // LANES
    loss_scale = 1.0 / math.sqrt(tokens)
    quarter_units = up_factor.shape[1]
    units = quarter_units * N_HID
    mix_row = mix_order[None, :]
    shape = jax.ShapeDtypeStruct
    pieces = shape((piece_rows, LANES), BF16)
    spread = pltpu.VMEM((piece_rows, LANES), F32)
    buffer = pltpu.VMEM((piece_rows, LANES), BF16)
    flops = 2 * units * BS * count
    small = 2 * BS * BS * count
    two_sems = pltpu.SemaphoreType.DMA((2,))

    first_out, weights, x_own, rows = call(
        first_kernel,
        (inputs, first_factor, up_factor, down_factor, row_order.reshape(-1, LANES)),
        (
            pieces,
            shape((2 * quarter_units, BS), BF16),
            shape((count, BS), BF16),
            shape((count // LANES, LANES), jnp.int32),
        ),
        [
            pltpu.VMEM((count, BS), BF16),
            pltpu.VMEM((1, BS, BS), BF16),
            pltpu.VMEM((2 * quarter_units, BS), BF16),
            pltpu.VMEM((count // LANES, LANES), jnp.int32),
            spread,
            buffer,
            pltpu.SemaphoreType.DMA((10,)),
        ],
        small,
        [HBM] * 5,
        [HBM] * 4,
    )
    far = from_partner(weights, 2)
    arrived = exchange(first_out)

    teacher = targets.at[rows.reshape(count)].get(mode="promise_in_bounds", wrap_negative_indices=False)
    weights, far, teacher = lax.optimization_barrier((weights, far, teacher))
    near, other = from_partner(weights, 1), from_partner(far, 1)
    (teacher_t,) = call(turn_kernel, (teacher,), (shape((BS, count), BF16),), [], small)
    up_mixed, down_t, up_mixed_t, down = call(
        prepare_kernel,
        (weights, far, near, other, mix_row),
        (
            shape((units, BS), BF16),
            shape((BS, units), BF16),
            shape((BS, units), BF16),
            shape((units, BS), BF16),
        ),
        [pltpu.VMEM((BS, units), BF16), pltpu.VMEM((units, BS), BF16), two_sems],
        small,
        out_specs=[VMEM, VMEM, HBM, HBM],
    )
    teacher_t, arrived = lax.optimization_barrier((teacher_t, arrived))

    summed, slope, hidden = call(
        forward_kernel,
        (arrived, up_mixed, down_t),
        (pieces, shape((units, count), F32), shape((units, count), BF16)),
        [spread, spread],
        2 * flops,
    )
    returned = exchange(summed)

    grad_returned, grad_last = call(
        functools.partial(error_kernel, loss_scale),
        (returned, last_factor, teacher_t),
        (pieces, shape((BS, BS), F32)),
        [spread, spread],
        3 * small,
    )
    grad_arrived = exchange(grad_returned)

    half_rows = shape((units + BS, BS), F32)
    grad_grouped, mine, theirs = call(
        backward_kernel,
        (grad_arrived, down, up_mixed_t, slope, hidden, arrived, grad_last),
        (pieces, half_rows, half_rows),
        [spread, spread, buffer, two_sems],
        4 * flops,
        out_specs=[HBM, VMEM, VMEM],
    )
    grad_first_out = exchange(grad_grouped)

    quarter_rows = shape((units // 2 + BS, BS), F32)
    mine, theirs = call(
        chip_sum_kernel, (mine, from_partner(theirs, 1)), (quarter_rows, quarter_rows), [], 0
    )
    factor_grad = shape((1, quarter_units, BS), F32)
    grad_up, grad_down, grad_last = call(
        totals_kernel,
        (mine, from_partner(theirs, 2), mix_row),
        (factor_grad, factor_grad, shape((1, BS, BS), F32)),
        [],
        0,
        pin=False,
    )

    (grad_first,) = call(
        last_kernel, (grad_first_out, x_own), (shape((BS, BS), BF16),), [spread], small
    )
    grad_first = sum_over_hid(grad_first)
    return (grad_first[None], grad_up, grad_down, grad_last)


def solution(mesh):
    placed = (
        P(None, "blk"),
        P(None, "blk"),
        P(),
        P(),
        P("blk", None, None),
        P("blk", "hid", None),
        P("blk", "hid", None),
        P("blk", None, None),
    )
    return jax.shard_map(
        local,
        mesh=mesh,
        in_specs=placed,
        out_specs=(
            P("blk", None, None),
            P("blk", "hid", None),
            P("blk", "hid", None),
            P("blk", None, None),
        ),
        check_vma=False,
    )
```

```python
import functools
import math

import jax
import jax.numpy as jnp
from jax import lax
from jax.experimental import pallas as pl
from jax.experimental.pallas import tpu as pltpu
from jax.sharding import PartitionSpec as P

BS = 128
NB = 64
N_HID = 4
LANES = 128
STEP = 1024
LEADER = 53


def token_groups():
    order = list(range(NB))
    order[0], order[LEADER] = LEADER, 0
    return [[b * N_HID + (q ^ (2 * (b % 2))) for b in order] for q in range(N_HID)]


def from_partner(value, m):
    return lax.ppermute(value, "hid", [(i, i ^ m) for i in range(N_HID)])


def exchange(rows):
    pieces = rows.reshape(NB, rows.shape[0] // NB, LANES)
    pieces = lax.all_to_all(
        pieces, ("blk", "hid"), 0, 0, tiled=True, axis_index_groups=token_groups()
    )
    return pieces.reshape(rows.shape)


def dot(a, b, dims):
    return lax.dot_general(a, b, (dims, ((), ())), preferred_element_type=jnp.float32)


def mm(a, b):
    return dot(a, b, ((1,), (0,)))


def sum_over_hid(part):
    got = [from_partner(part, m).astype(jnp.float32) for m in (1, 2, 3)]
    return (part.astype(jnp.float32) + got[0]) + (got[1] + got[2])


def own_quarter():
    return lax.axis_index("hid") ^ (2 * (lax.axis_index("blk") % 2))


def put_pieces(spread, value, at):
    chunks = spread.shape[0] // BS
    for j in range(value.shape[1] // LANES):
        spread[pl.ds(at // LANES + j, BS, chunks), :] = value[:, j * LANES : (j + 1) * LANES]


def get_pieces(spread, at, size):
    chunks = spread.shape[0] // BS
    parts = [spread[pl.ds(at // LANES + j, BS, chunks), :] for j in range(size // LANES)]
    return jnp.concatenate(parts, axis=1).astype(jnp.bfloat16)


def trade_leader(spread):
    size = spread.shape[0] // NB
    leader = spread[LEADER * size : (LEADER + 1) * size, :]
    spread[LEADER * size : (LEADER + 1) * size, :] = spread[0:size, :]
    spread[0:size, :] = leader


def take_in(spread, ref):
    spread[...] = ref[...].astype(jnp.float32)
    trade_leader(spread)


def send_out(spread, buffer, hbm, sems, first_sem):
    trade_leader(spread)
    half = spread.shape[0] // 2
    copies = []
    for i in range(2):
        rows = pl.ds(i * half, half)
        buffer[rows, :] = spread[rows, :].astype(jnp.bfloat16)
        copies.append(pltpu.make_async_copy(buffer.at[rows], hbm.at[rows], sems.at[first_sem + i]))
        copies[-1].start()
    return copies


def first_kernel(
    x_hbm, first_hbm, up_hbm, down_hbm, order_hbm, out_hbm, packed_hbm, x_own_hbm, rows_hbm,
    x, first, packed, rows, spread, buffer, sems,
):
    count = x.shape[0]
    units = up_hbm.shape[1]
    order_rows = rows.shape[0]
    start = pl.multiple_of(own_quarter() * count, count)
    order_start = pl.multiple_of(own_quarter() * order_rows, order_rows)
    fetch = [
        (x_hbm.at[pl.ds(start, count)], x),
        (first_hbm, first),
        (up_hbm.at[0], packed.at[pl.ds(0, units)]),
        (down_hbm.at[0], packed.at[pl.ds(units, units)]),
        (order_hbm.at[pl.ds(order_start, order_rows)], rows),
    ]
    fetch = [pltpu.make_async_copy(a, b, sems.at[i]) for i, (a, b) in enumerate(fetch)]
    for copy in fetch:
        copy.start()
    fetch[1].wait()
    first_t = first[0].T
    fetch[0].wait()
    put_pieces(spread, dot(first_t, x[...], ((1,), (1,))), 0)
    copies = send_out(spread, buffer, out_hbm, sems, 5)
    for copy in fetch[2:]:
        copy.wait()
    for i, (source, target) in enumerate(((x, x_own_hbm), (packed, packed_hbm), (rows, rows_hbm))):
        copies.append(pltpu.make_async_copy(source, target, sems.at[7 + i]))
        copies[-1].start()
    for copy in copies:
        copy.wait()


def unit_matrix():
    ids = lax.broadcasted_iota(jnp.int32, (BS, BS), 0)
    eye = (lax.broadcasted_iota(jnp.int32, (BS, BS), 1) == ids).astype(jnp.float32)
    return eye.astype(jnp.bfloat16)


def prepare_kernel(
    own_ref, far_ref, near_ref, other_ref, mix_ref, up_ref, down_t_ref, up_t_hbm, down_hbm, up_t, down, sems
):
    units = own_ref.shape[0] // 2
    refs = (own_ref, far_ref, near_ref, other_ref)
    ids = lax.broadcasted_iota(jnp.int32, (BS, BS), 0)
    one_hot = (mix_ref[...] == ids).astype(jnp.float32).astype(jnp.bfloat16)
    for i, ref in enumerate(refs):
        down[i * units : (i + 1) * units, :] = ref[units:, :]
    copies = [pltpu.make_async_copy(down, down_hbm, sems.at[0])]
    copies[0].start()
    up = jnp.concatenate([ref[0:units, :] for ref in refs])
    up_t[...] = dot(one_hot, up, ((1,), (1,))).astype(jnp.bfloat16)
    copies.append(pltpu.make_async_copy(up_t, up_t_hbm, sems.at[1]))
    copies[1].start()
    up_ref[...] = dot(up, one_hot, ((1,), (1,))).astype(jnp.bfloat16)
    down_t_ref[...] = dot(unit_matrix(), down[...], ((1,), (1,))).astype(jnp.bfloat16)
    for copy in copies:
        copy.wait()


def turn_kernel(in_ref, out_ref):
    out_ref[...] = dot(unit_matrix(), in_ref[...], ((1,), (1,))).astype(jnp.bfloat16)


def forward_kernel(
    in_ref, up_ref, down_t_ref, out_ref, slope_ref, hidden_ref, spread_in, spread
):
    take_in(spread_in, in_ref)
    up = up_ref[...]
    down_t = down_t_ref[...]
    for at in range(0, hidden_ref.shape[1], STEP):
        preact = mm(up, get_pieces(spread_in, at, STEP))
        cdf = 0.5 * (1.0 + lax.erf(preact * (1.0 / math.sqrt(2.0))))
        dens = jnp.exp(-0.5 * preact * preact) * (1.0 / math.sqrt(2.0 * math.pi))
        hidden = (preact * cdf).astype(jnp.bfloat16)
        hidden_ref[:, at : at + STEP] = hidden
        slope_ref[:, at : at + STEP] = cdf + preact * dens
        put_pieces(spread, mm(down_t, hidden), at)
    trade_leader(spread)
    out_ref[...] = spread[...].astype(jnp.bfloat16)


def error_kernel(scale, in_ref, last_ref, teacher_ref, out_ref, grad_ref, spread_in, spread):
    take_in(spread_in, in_ref)
    last = last_ref[0]
    last_t = last.T
    grad_last = None
    for at in range(0, teacher_ref.shape[1], STEP):
        returned = get_pieces(spread_in, at, STEP)
        teacher = teacher_ref[:, at : at + STEP].astype(jnp.float32)
        err = ((mm(last_t, returned) - teacher) * scale).astype(jnp.bfloat16)
        put_pieces(spread, mm(last, err), at)
        part = dot(returned, err, ((1,), (1,)))
        grad_last = part if grad_last is None else grad_last + part
    trade_leader(spread)
    out_ref[...] = spread[...].astype(jnp.bfloat16)
    grad_ref[...] = grad_last


def backward_kernel(
    in_ref, down_ref, up_t_ref, slope_ref, hidden_ref, arrived_ref, last_ref,
    out_hbm, mine_ref, theirs_ref, spread_in, spread, buffer, sems,
):
    units, count = hidden_ref.shape
    half = units // 2
    take_in(spread_in, in_ref)
    grad_out = get_pieces(spread_in, 0, count)
    grad_hidden = mm(down_ref[...], grad_out)
    grad = (grad_hidden * slope_ref[...]).astype(jnp.bfloat16)
    put_pieces(spread, mm(up_t_ref[...], grad), 0)
    copies = send_out(spread, buffer, out_hbm, sems, 0)
    mine_ref[units:, :] = last_ref[...]
    theirs_ref[units:, :] = last_ref[...]
    down = dot(hidden_ref[...], grad_out, ((1,), (1,)))
    mine_ref[half:units, :] = down[:half]
    theirs_ref[half:units, :] = down[half:]
    take_in(spread_in, arrived_ref)
    up = dot(grad, get_pieces(spread_in, 0, count), ((1,), (1,)))
    mine_ref[0:half, :] = up[:half]
    theirs_ref[0:half, :] = up[half:]
    for copy in copies:
        copy.wait()


def chip_sum_kernel(mine_ref, got_ref, mine_out, theirs_out):
    quarter = (mine_ref.shape[0] - BS) // 4
    total = mine_ref[...] + got_ref[...]
    mine_out[0:quarter, :] = total[0:quarter]
    theirs_out[0:quarter, :] = total[quarter : 2 * quarter]
    mine_out[quarter : 2 * quarter, :] = total[2 * quarter : 3 * quarter]
    theirs_out[quarter : 2 * quarter, :] = total[3 * quarter : 4 * quarter]
    mine_out[2 * quarter :, :] = total[4 * quarter :]
    theirs_out[2 * quarter :, :] = total[4 * quarter :]


def totals_kernel(mine_ref, got_ref, mix_ref, up_ref, down_ref, last_ref):
    quarter = up_ref.shape[1]
    total = mine_ref[...] + got_ref[...]
    ids = lax.broadcasted_iota(jnp.int32, (BS, BS), 0)
    one_hot = (mix_ref[...] == ids).astype(jnp.float32)
    up_ref[0] = jnp.dot(
        total[0:quarter], one_hot, precision=lax.Precision.HIGHEST, preferred_element_type=jnp.float32
    )
    down_ref[0] = total[quarter : 2 * quarter]
    last_ref[0] = total[2 * quarter :]


def last_kernel(in_ref, x_ref, out_ref, spread_in):
    take_in(spread_in, in_ref)
    grad = get_pieces(spread_in, 0, x_ref.shape[0])
    out_ref[...] = mm(grad, x_ref[...]).T.astype(jnp.bfloat16)


VMEM = pl.BlockSpec(memory_space=pltpu.VMEM)
HBM = pl.BlockSpec(memory_space=pltpu.HBM)
BF16 = jnp.bfloat16
F32 = jnp.float32


def call(kernel, ins, outs, scratch, flops, in_specs=None, out_specs=None, pin=True):
    moved = sum(a.size * a.dtype.itemsize for a in ins) + sum(
        math.prod(o.shape) * o.dtype.itemsize for o in outs
    )
    if in_specs:
        ins = [
            pltpu.with_memory_space_constraint(a, pltpu.HBM) if spec is HBM else a
            for a, spec in zip(ins, in_specs)
        ]
    places = out_specs or [VMEM] * len(outs)
    if pin:
        outs = tuple(
            (pltpu.HBM if spec is HBM else pltpu.VMEM)(o.shape, o.dtype) for o, spec in zip(outs, places)
        )
    return pl.pallas_call(
        kernel,
        out_shape=outs,
        in_specs=in_specs or [VMEM] * len(ins),
        out_specs=out_specs or [VMEM] * len(outs),
        scratch_shapes=scratch,
        compiler_params=pltpu.CompilerParams(vmem_limit_bytes=16 * 1024 * 1024),
        cost_estimate=pl.CostEstimate(flops=flops, bytes_accessed=moved, transcendentals=0),
    )(*ins)


def local(inputs, targets, row_order, mix_order, first_factor, up_factor, down_factor, last_factor):
    tokens = inputs.shape[0]
    count = tokens // N_HID
    steps = count // STEP
    piece_rows = BS * count // LANES
    loss_scale = 1.0 / math.sqrt(tokens)
    quarter_units = up_factor.shape[1]
    units = quarter_units * N_HID
    mix_row = mix_order[None, :]
    shape = jax.ShapeDtypeStruct
    pieces = shape((piece_rows, LANES), BF16)
    spread = pltpu.VMEM((piece_rows, LANES), F32)
    buffer = pltpu.VMEM((piece_rows, LANES), BF16)
    flops = 2 * units * BS * count
    small = 2 * BS * BS * count
    two_sems = pltpu.SemaphoreType.DMA((2,))

    first_out, weights, x_own, rows = call(
        first_kernel,
        (inputs, first_factor, up_factor, down_factor, row_order.reshape(-1, LANES)),
        (
            pieces,
            shape((2 * quarter_units, BS), BF16),
            shape((count, BS), BF16),
            shape((count // LANES, LANES), jnp.int32),
        ),
        [
            pltpu.VMEM((count, BS), BF16),
            pltpu.VMEM((1, BS, BS), BF16),
            pltpu.VMEM((2 * quarter_units, BS), BF16),
            pltpu.VMEM((count // LANES, LANES), jnp.int32),
            spread,
            buffer,
            pltpu.SemaphoreType.DMA((10,)),
        ],
        small,
        [HBM] * 5,
        [HBM] * 4,
    )
    far = from_partner(weights, 2)
    arrived = exchange(first_out)

    teacher = targets.at[rows.reshape(count)].get(mode="promise_in_bounds", wrap_negative_indices=False)
    weights, far, teacher = lax.optimization_barrier((weights, far, teacher))
    near, other = from_partner(weights, 1), from_partner(far, 1)
    (teacher_t,) = call(turn_kernel, (teacher,), (shape((BS, count), BF16),), [], small)
    up_mixed, down_t, up_mixed_t, down = call(
        prepare_kernel,
        (weights, far, near, other, mix_row),
        (
            shape((units, BS), BF16),
            shape((BS, units), BF16),
            shape((BS, units), BF16),
            shape((units, BS), BF16),
        ),
        [pltpu.VMEM((BS, units), BF16), pltpu.VMEM((units, BS), BF16), two_sems],
        small,
        out_specs=[VMEM, VMEM, HBM, HBM],
    )
    teacher_t, arrived = lax.optimization_barrier((teacher_t, arrived))

    summed, slope, hidden = call(
        forward_kernel,
        (arrived, up_mixed, down_t),
        (pieces, shape((units, count), F32), shape((units, count), BF16)),
        [spread, spread],
        2 * flops,
    )
    returned = exchange(summed)

    grad_returned, grad_last = call(
        functools.partial(error_kernel, loss_scale),
        (returned, last_factor, teacher_t),
        (pieces, shape((BS, BS), F32)),
        [spread, spread],
        3 * small,
    )
    grad_arrived = exchange(grad_returned)

    half_rows = shape((units + BS, BS), F32)
    grad_grouped, mine, theirs = call(
        backward_kernel,
        (grad_arrived, down, up_mixed_t, slope, hidden, arrived, grad_last),
        (pieces, half_rows, half_rows),
        [spread, spread, buffer, two_sems],
        4 * flops,
        out_specs=[HBM, VMEM, VMEM],
    )
    grad_first_out = exchange(grad_grouped)

    quarter_rows = shape((units // 2 + BS, BS), F32)
    mine, theirs = call(
        chip_sum_kernel, (mine, from_partner(theirs, 1)), (quarter_rows, quarter_rows), [], 0
    )
    factor_grad = shape((1, quarter_units, BS), F32)
    grad_up, grad_down, grad_last = call(
        totals_kernel,
        (mine, from_partner(theirs, 2), mix_row),
        (factor_grad, factor_grad, shape((1, BS, BS), F32)),
        [],
        0,
        pin=False,
    )

    (grad_first,) = call(
        last_kernel, (grad_first_out, x_own), (shape((BS, BS), BF16),), [spread], small
    )
    grad_first = sum_over_hid(grad_first)
    return (grad_first[None], grad_up, grad_down, grad_last)


def solution(mesh):
    placed = (
        P(None, "blk"),
        P(None, "blk"),
        P(),
        P(),
        P("blk", None, None),
        P("blk", "hid", None),
        P("blk", "hid", None),
        P("blk", None, None),
    )
    return jax.shard_map(
        local,
        mesh=mesh,
        in_specs=placed,
        out_specs=(
            P("blk", None, None),
            P("blk", "hid", None),
            P("blk", "hid", None),
            P("blk", None, None),
        ),
        check_vma=False,
    )
```

```python
import functools
import math

import jax
import jax.numpy as jnp
from jax import lax
from jax.experimental import pallas as pl
from jax.experimental.pallas import tpu as pltpu
from jax.sharding import PartitionSpec as P

BS = 128
NB = 64
N_HID = 4
LANES = 128
STEP = 1024
LEADERS = (45, 53, 53, 53)


def token_groups(leader):
    order = list(range(NB))
    order[0], order[leader] = leader, 0
    return [[b * N_HID + (q ^ (2 * (b % 2))) for b in order] for q in range(N_HID)]


def from_partner(value, m):
    return lax.ppermute(value, "hid", [(i, i ^ m) for i in range(N_HID)])


def exchange(rows, step):
    pieces = rows.reshape(NB, rows.shape[0] // NB, LANES)
    pieces = lax.all_to_all(
        pieces, ("blk", "hid"), 0, 0, tiled=True, axis_index_groups=token_groups(LEADERS[step])
    )
    return pieces.reshape(rows.shape)


def dot(a, b, dims):
    return lax.dot_general(a, b, (dims, ((), ())), preferred_element_type=jnp.float32)


def mm(a, b):
    return dot(a, b, ((1,), (0,)))


def sum_over_hid(part):
    got = [from_partner(part, m).astype(jnp.float32) for m in (1, 2, 3)]
    return (part.astype(jnp.float32) + got[0]) + (got[1] + got[2])


def own_quarter():
    return lax.axis_index("hid") ^ (2 * (lax.axis_index("blk") % 2))


def put_pieces(spread, value, at):
    chunks = spread.shape[0] // BS
    for j in range(value.shape[1] // LANES):
        spread[pl.ds(at // LANES + j, BS, chunks), :] = value[:, j * LANES : (j + 1) * LANES]


def get_pieces(spread, at, size):
    chunks = spread.shape[0] // BS
    parts = [spread[pl.ds(at // LANES + j, BS, chunks), :] for j in range(size // LANES)]
    return jnp.concatenate(parts, axis=1).astype(jnp.bfloat16)


def trade_leader(spread, step):
    size = spread.shape[0] // NB
    at = LEADERS[step] * size
    leader = spread[at : at + size, :]
    spread[at : at + size, :] = spread[0:size, :]
    spread[0:size, :] = leader


def take_in(spread, ref, step):
    spread[...] = ref[...].astype(jnp.float32)
    trade_leader(spread, step)


def send_out(spread, buffer, hbm, sems, first_sem, step):
    trade_leader(spread, step)
    half = spread.shape[0] // 2
    copies = []
    for i in range(2):
        rows = pl.ds(i * half, half)
        buffer[rows, :] = spread[rows, :].astype(jnp.bfloat16)
        copies.append(pltpu.make_async_copy(buffer.at[rows], hbm.at[rows], sems.at[first_sem + i]))
        copies[-1].start()
    return copies


def first_kernel(
    x_hbm, first_hbm, up_hbm, down_hbm, order_hbm, out_hbm, packed_hbm, x_own_hbm, rows_hbm,
    x, first, packed, rows, spread, buffer, sems,
):
    count = x.shape[0]
    units = up_hbm.shape[1]
    order_rows = rows.shape[0]
    start = pl.multiple_of(own_quarter() * count, count)
    order_start = pl.multiple_of(own_quarter() * order_rows, order_rows)
    fetch = [
        (x_hbm.at[pl.ds(start, count)], x),
        (first_hbm, first),
        (up_hbm.at[0], packed.at[pl.ds(0, units)]),
        (down_hbm.at[0], packed.at[pl.ds(units, units)]),
        (order_hbm.at[pl.ds(order_start, order_rows)], rows),
    ]
    fetch = [pltpu.make_async_copy(a, b, sems.at[i]) for i, (a, b) in enumerate(fetch)]
    for copy in fetch:
        copy.start()
    fetch[1].wait()
    first_t = first[0].T
    fetch[0].wait()
    put_pieces(spread, dot(first_t, x[...], ((1,), (1,))), 0)
    copies = send_out(spread, buffer, out_hbm, sems, 5, 0)
    for copy in fetch[2:]:
        copy.wait()
    for i, (source, target) in enumerate(((x, x_own_hbm), (packed, packed_hbm), (rows, rows_hbm))):
        copies.append(pltpu.make_async_copy(source, target, sems.at[7 + i]))
        copies[-1].start()
    for copy in copies:
        copy.wait()


def unit_matrix():
    ids = lax.broadcasted_iota(jnp.int32, (BS, BS), 0)
    eye = (lax.broadcasted_iota(jnp.int32, (BS, BS), 1) == ids).astype(jnp.float32)
    return eye.astype(jnp.bfloat16)


def prepare_kernel(
    own_ref, far_ref, near_ref, other_ref, mix_ref, up_ref, down_t_ref, up_t_hbm, down_hbm, up_t, down, sems
):
    units = own_ref.shape[0] // 2
    refs = (own_ref, far_ref, near_ref, other_ref)
    ids = lax.broadcasted_iota(jnp.int32, (BS, BS), 0)
    one_hot = (mix_ref[...] == ids).astype(jnp.float32).astype(jnp.bfloat16)
    for i, ref in enumerate(refs):
        down[i * units : (i + 1) * units, :] = ref[units:, :]
    copies = [pltpu.make_async_copy(down, down_hbm, sems.at[0])]
    copies[0].start()
    up = jnp.concatenate([ref[0:units, :] for ref in refs])
    up_t[...] = dot(one_hot, up, ((1,), (1,))).astype(jnp.bfloat16)
    copies.append(pltpu.make_async_copy(up_t, up_t_hbm, sems.at[1]))
    copies[1].start()
    up_ref[...] = dot(up, one_hot, ((1,), (1,))).astype(jnp.bfloat16)
    down_t_ref[...] = dot(unit_matrix(), down[...], ((1,), (1,))).astype(jnp.bfloat16)
    for copy in copies:
        copy.wait()


def turn_kernel(in_ref, out_ref):
    out_ref[...] = dot(unit_matrix(), in_ref[...], ((1,), (1,))).astype(jnp.bfloat16)


def forward_kernel(
    in_ref, up_ref, down_t_ref, out_ref, slope_ref, hidden_ref, spread_in, spread
):
    take_in(spread_in, in_ref, 0)
    up = up_ref[...]
    down_t = down_t_ref[...]
    for at in range(0, hidden_ref.shape[1], STEP):
        preact = mm(up, get_pieces(spread_in, at, STEP))
        cdf = 0.5 * (1.0 + lax.erf(preact * (1.0 / math.sqrt(2.0))))
        dens = jnp.exp(-0.5 * preact * preact) * (1.0 / math.sqrt(2.0 * math.pi))
        hidden = (preact * cdf).astype(jnp.bfloat16)
        hidden_ref[:, at : at + STEP] = hidden
        slope_ref[:, at : at + STEP] = cdf + preact * dens
        put_pieces(spread, mm(down_t, hidden), at)
    trade_leader(spread, 1)
    out_ref[...] = spread[...].astype(jnp.bfloat16)


def error_kernel(scale, in_ref, last_ref, teacher_ref, out_ref, grad_ref, spread_in, spread):
    take_in(spread_in, in_ref, 1)
    last = last_ref[0]
    last_t = last.T
    grad_last = None
    for at in range(0, teacher_ref.shape[1], STEP):
        returned = get_pieces(spread_in, at, STEP)
        teacher = teacher_ref[:, at : at + STEP].astype(jnp.float32)
        err = ((mm(last_t, returned) - teacher) * scale).astype(jnp.bfloat16)
        put_pieces(spread, mm(last, err), at)
        part = dot(returned, err, ((1,), (1,)))
        grad_last = part if grad_last is None else grad_last + part
    trade_leader(spread, 2)
    out_ref[...] = spread[...].astype(jnp.bfloat16)
    grad_ref[...] = grad_last


def backward_kernel(
    in_ref, down_ref, up_t_ref, slope_ref, hidden_ref, arrived_ref, last_ref,
    out_hbm, mine_ref, theirs_ref, spread_in, spread, buffer, sems,
):
    units, count = hidden_ref.shape
    half = units // 2
    take_in(spread_in, in_ref, 2)
    grad_out = get_pieces(spread_in, 0, count)
    grad_hidden = mm(down_ref[...], grad_out)
    grad = (grad_hidden * slope_ref[...]).astype(jnp.bfloat16)
    put_pieces(spread, mm(up_t_ref[...], grad), 0)
    copies = send_out(spread, buffer, out_hbm, sems, 0, 3)
    mine_ref[units:, :] = last_ref[...]
    theirs_ref[units:, :] = last_ref[...]
    down = dot(hidden_ref[...], grad_out, ((1,), (1,)))
    mine_ref[half:units, :] = down[:half]
    theirs_ref[half:units, :] = down[half:]
    take_in(spread_in, arrived_ref, 0)
    up = dot(grad, get_pieces(spread_in, 0, count), ((1,), (1,)))
    mine_ref[0:half, :] = up[:half]
    theirs_ref[0:half, :] = up[half:]
    for copy in copies:
        copy.wait()


def chip_sum_kernel(mine_ref, got_ref, mine_out, theirs_out):
    quarter = (mine_ref.shape[0] - BS) // 4
    total = mine_ref[...] + got_ref[...]
    mine_out[0:quarter, :] = total[0:quarter]
    theirs_out[0:quarter, :] = total[quarter : 2 * quarter]
    mine_out[quarter : 2 * quarter, :] = total[2 * quarter : 3 * quarter]
    theirs_out[quarter : 2 * quarter, :] = total[3 * quarter : 4 * quarter]
    mine_out[2 * quarter :, :] = total[4 * quarter :]
    theirs_out[2 * quarter :, :] = total[4 * quarter :]


def totals_kernel(mine_ref, got_ref, mix_ref, up_ref, down_ref, last_ref):
    quarter = up_ref.shape[1]
    total = mine_ref[...] + got_ref[...]
    ids = lax.broadcasted_iota(jnp.int32, (BS, BS), 0)
    one_hot = (mix_ref[...] == ids).astype(jnp.float32)
    up_ref[0] = jnp.dot(
        total[0:quarter], one_hot, precision=lax.Precision.HIGHEST, preferred_element_type=jnp.float32
    )
    down_ref[0] = total[quarter : 2 * quarter]
    last_ref[0] = total[2 * quarter :]


def last_kernel(in_ref, x_ref, out_ref, spread_in):
    take_in(spread_in, in_ref, 3)
    grad = get_pieces(spread_in, 0, x_ref.shape[0])
    out_ref[...] = mm(grad, x_ref[...]).T.astype(jnp.bfloat16)


VMEM = pl.BlockSpec(memory_space=pltpu.VMEM)
HBM = pl.BlockSpec(memory_space=pltpu.HBM)
BF16 = jnp.bfloat16
F32 = jnp.float32


def call(kernel, ins, outs, scratch, flops, in_specs=None, out_specs=None, pin=True):
    moved = sum(a.size * a.dtype.itemsize for a in ins) + sum(
        math.prod(o.shape) * o.dtype.itemsize for o in outs
    )
    if in_specs:
        ins = [
            pltpu.with_memory_space_constraint(a, pltpu.HBM) if spec is HBM else a
            for a, spec in zip(ins, in_specs)
        ]
    places = out_specs or [VMEM] * len(outs)
    if pin:
        outs = tuple(
            (pltpu.HBM if spec is HBM else pltpu.VMEM)(o.shape, o.dtype) for o, spec in zip(outs, places)
        )
    return pl.pallas_call(
        kernel,
        out_shape=outs,
        in_specs=in_specs or [VMEM] * len(ins),
        out_specs=out_specs or [VMEM] * len(outs),
        scratch_shapes=scratch,
        compiler_params=pltpu.CompilerParams(vmem_limit_bytes=16 * 1024 * 1024),
        cost_estimate=pl.CostEstimate(flops=flops, bytes_accessed=moved, transcendentals=0),
    )(*ins)


def local(inputs, targets, row_order, mix_order, first_factor, up_factor, down_factor, last_factor):
    tokens = inputs.shape[0]
    count = tokens // N_HID
    steps = count // STEP
    piece_rows = BS * count // LANES
    loss_scale = 1.0 / math.sqrt(tokens)
    quarter_units = up_factor.shape[1]
    units = quarter_units * N_HID
    mix_row = mix_order[None, :]
    shape = jax.ShapeDtypeStruct
    pieces = shape((piece_rows, LANES), BF16)
    spread = pltpu.VMEM((piece_rows, LANES), F32)
    buffer = pltpu.VMEM((piece_rows, LANES), BF16)
    flops = 2 * units * BS * count
    small = 2 * BS * BS * count
    two_sems = pltpu.SemaphoreType.DMA((2,))

    first_out, weights, x_own, rows = call(
        first_kernel,
        (inputs, first_factor, up_factor, down_factor, row_order.reshape(-1, LANES)),
        (
            pieces,
            shape((2 * quarter_units, BS), BF16),
            shape((count, BS), BF16),
            shape((count // LANES, LANES), jnp.int32),
        ),
        [
            pltpu.VMEM((count, BS), BF16),
            pltpu.VMEM((1, BS, BS), BF16),
            pltpu.VMEM((2 * quarter_units, BS), BF16),
            pltpu.VMEM((count // LANES, LANES), jnp.int32),
            spread,
            buffer,
            pltpu.SemaphoreType.DMA((10,)),
        ],
        small,
        [HBM] * 5,
        [HBM] * 4,
    )
    far = from_partner(weights, 2)
    arrived = exchange(first_out, 0)

    teacher = targets.at[rows.reshape(count)].get(mode="promise_in_bounds", wrap_negative_indices=False)
    weights, far, teacher = lax.optimization_barrier((weights, far, teacher))
    near, other = from_partner(weights, 1), from_partner(far, 1)
    (teacher_t,) = call(turn_kernel, (teacher,), (shape((BS, count), BF16),), [], small)
    up_mixed, down_t, up_mixed_t, down = call(
        prepare_kernel,
        (weights, far, near, other, mix_row),
        (
            shape((units, BS), BF16),
            shape((BS, units), BF16),
            shape((BS, units), BF16),
            shape((units, BS), BF16),
        ),
        [pltpu.VMEM((BS, units), BF16), pltpu.VMEM((units, BS), BF16), two_sems],
        small,
        out_specs=[VMEM, VMEM, HBM, HBM],
    )
    teacher_t, arrived = lax.optimization_barrier((teacher_t, arrived))

    summed, slope, hidden = call(
        forward_kernel,
        (arrived, up_mixed, down_t),
        (pieces, shape((units, count), F32), shape((units, count), BF16)),
        [spread, spread],
        2 * flops,
    )
    returned = exchange(summed, 1)

    grad_returned, grad_last = call(
        functools.partial(error_kernel, loss_scale),
        (returned, last_factor, teacher_t),
        (pieces, shape((BS, BS), F32)),
        [spread, spread],
        3 * small,
    )
    grad_arrived = exchange(grad_returned, 2)

    half_rows = shape((units + BS, BS), F32)
    grad_grouped, mine, theirs = call(
        backward_kernel,
        (grad_arrived, down, up_mixed_t, slope, hidden, arrived, grad_last),
        (pieces, half_rows, half_rows),
        [spread, spread, buffer, two_sems],
        4 * flops,
        out_specs=[HBM, VMEM, VMEM],
    )
    grad_first_out = exchange(grad_grouped, 3)

    quarter_rows = shape((units // 2 + BS, BS), F32)
    mine, theirs = call(
        chip_sum_kernel, (mine, from_partner(theirs, 1)), (quarter_rows, quarter_rows), [], 0
    )
    factor_grad = shape((1, quarter_units, BS), F32)
    grad_up, grad_down, grad_last = call(
        totals_kernel,
        (mine, from_partner(theirs, 2), mix_row),
        (factor_grad, factor_grad, shape((1, BS, BS), F32)),
        [],
        0,
        pin=False,
    )

    (grad_first,) = call(
        last_kernel, (grad_first_out, x_own), (shape((BS, BS), BF16),), [spread], small
    )
    grad_first = sum_over_hid(grad_first)
    return (grad_first[None], grad_up, grad_down, grad_last)


def solution(mesh):
    placed = (
        P(None, "blk"),
        P(None, "blk"),
        P(),
        P(),
        P("blk", None, None),
        P("blk", "hid", None),
        P("blk", "hid", None),
        P("blk", None, None),
    )
    return jax.shard_map(
        local,
        mesh=mesh,
        in_specs=placed,
        out_specs=(
            P("blk", None, None),
            P("blk", "hid", None),
            P("blk", "hid", None),
            P("blk", None, None),
        ),
        check_vma=False,
    )
```

```python
import functools
import math

import jax
import jax.numpy as jnp
from jax import lax
from jax.experimental import pallas as pl
from jax.experimental.pallas import tpu as pltpu
from jax.sharding import PartitionSpec as P

BS = 128
NB = 64
N_HID = 4
LANES = 128
STEP = 1024
LEADERS = (45, 53, 53, 53)


def token_groups(leader):
    order = list(range(NB))
    order[0], order[leader] = leader, 0
    return [[b * N_HID + (q ^ (2 * (b % 2))) for b in order] for q in range(N_HID)]


def from_partner(value, m):
    return lax.ppermute(value, "hid", [(i, i ^ m) for i in range(N_HID)])


def exchange(rows, step):
    pieces = rows.reshape(NB, rows.shape[0] // NB, LANES)
    pieces = lax.all_to_all(
        pieces, ("blk", "hid"), 0, 0, tiled=True, axis_index_groups=token_groups(LEADERS[step])
    )
    return pieces.reshape(rows.shape)


def dot(a, b, dims):
    return lax.dot_general(a, b, (dims, ((), ())), preferred_element_type=jnp.float32)


def mm(a, b):
    return dot(a, b, ((1,), (0,)))


def sum_over_hid(part):
    got = [from_partner(part, m).astype(jnp.float32) for m in (1, 2, 3)]
    return (part.astype(jnp.float32) + got[0]) + (got[1] + got[2])


def own_quarter():
    return lax.axis_index("hid") ^ (2 * (lax.axis_index("blk") % 2))


def put_pieces(spread, value, at):
    chunks = spread.shape[0] // BS
    for j in range(value.shape[1] // LANES):
        spread[pl.ds(at // LANES + j, BS, chunks), :] = value[:, j * LANES : (j + 1) * LANES]


def get_pieces(spread, at, size):
    chunks = spread.shape[0] // BS
    parts = [spread[pl.ds(at // LANES + j, BS, chunks), :] for j in range(size // LANES)]
    return jnp.concatenate(parts, axis=1).astype(jnp.bfloat16)


def trade_leader(spread, step):
    size = spread.shape[0] // NB
    at = LEADERS[step] * size
    leader = spread[at : at + size, :]
    spread[at : at + size, :] = spread[0:size, :]
    spread[0:size, :] = leader


def take_in(spread, ref, step):
    spread[...] = ref[...].astype(jnp.float32)
    trade_leader(spread, step)


def send_out(spread, buffer, hbm, sems, first_sem, step):
    trade_leader(spread, step)
    half = spread.shape[0] // 2
    copies = []
    for i in range(2):
        rows = pl.ds(i * half, half)
        buffer[rows, :] = spread[rows, :].astype(jnp.bfloat16)
        copies.append(pltpu.make_async_copy(buffer.at[rows], hbm.at[rows], sems.at[first_sem + i]))
        copies[-1].start()
    return copies


def first_kernel(
    x_hbm, first_hbm, up_hbm, down_hbm, order_hbm, out_hbm, packed_hbm, x_own_hbm, rows_hbm,
    x, first, packed, rows, spread, buffer, sems,
):
    count = x.shape[0]
    units = up_hbm.shape[1]
    order_rows = rows.shape[0]
    start = pl.multiple_of(own_quarter() * count, count)
    order_start = pl.multiple_of(own_quarter() * order_rows, order_rows)
    fetch = [
        (x_hbm.at[pl.ds(start, count)], x),
        (first_hbm, first),
        (up_hbm.at[0], packed.at[pl.ds(0, units)]),
        (down_hbm.at[0], packed.at[pl.ds(units, units)]),
        (order_hbm.at[pl.ds(order_start, order_rows)], rows),
    ]
    fetch = [pltpu.make_async_copy(a, b, sems.at[i]) for i, (a, b) in enumerate(fetch)]
    for copy in fetch:
        copy.start()
    fetch[1].wait()
    first_t = first[0].T
    fetch[0].wait()
    put_pieces(spread, dot(first_t, x[...], ((1,), (1,))), 0)
    copies = send_out(spread, buffer, out_hbm, sems, 5, 0)
    for copy in fetch[2:]:
        copy.wait()
    for i, (source, target) in enumerate(((x, x_own_hbm), (packed, packed_hbm), (rows, rows_hbm))):
        copies.append(pltpu.make_async_copy(source, target, sems.at[7 + i]))
        copies[-1].start()
    for copy in copies:
        copy.wait()


def unit_matrix():
    ids = lax.broadcasted_iota(jnp.int32, (BS, BS), 0)
    eye = (lax.broadcasted_iota(jnp.int32, (BS, BS), 1) == ids).astype(jnp.float32)
    return eye.astype(jnp.bfloat16)


def prepare_kernel(
    own_ref, far_ref, near_ref, other_ref, mix_ref, up_ref, down_t_ref, up_t_hbm, down_hbm, up_t, down, sems
):
    units = own_ref.shape[0] // 2
    refs = (own_ref, far_ref, near_ref, other_ref)
    ids = lax.broadcasted_iota(jnp.int32, (BS, BS), 0)
    one_hot = (mix_ref[...] == ids).astype(jnp.float32).astype(jnp.bfloat16)
    for i, ref in enumerate(refs):
        down[i * units : (i + 1) * units, :] = ref[units:, :]
    copies = [pltpu.make_async_copy(down, down_hbm, sems.at[0])]
    copies[0].start()
    up = jnp.concatenate([ref[0:units, :] for ref in refs])
    up_t[...] = dot(one_hot, up, ((1,), (1,))).astype(jnp.bfloat16)
    copies.append(pltpu.make_async_copy(up_t, up_t_hbm, sems.at[1]))
    copies[1].start()
    up_ref[...] = dot(up, one_hot, ((1,), (1,))).astype(jnp.bfloat16)
    down_t_ref[...] = dot(unit_matrix(), down[...], ((1,), (1,))).astype(jnp.bfloat16)
    for copy in copies:
        copy.wait()


def turn_kernel(in_ref, out_ref):
    out_ref[...] = dot(unit_matrix(), in_ref[...], ((1,), (1,))).astype(jnp.bfloat16)


def forward_kernel(
    in_ref, up_ref, down_t_ref, out_ref, slope_ref, hidden_ref, spread_in, spread
):
    take_in(spread_in, in_ref, 0)
    up = up_ref[...]
    down_t = down_t_ref[...]
    for at in range(0, hidden_ref.shape[1], STEP):
        preact = mm(up, get_pieces(spread_in, at, STEP))
        cdf = 0.5 * (1.0 + lax.erf(preact * (1.0 / math.sqrt(2.0))))
        dens = jnp.exp(-0.5 * preact * preact) * (1.0 / math.sqrt(2.0 * math.pi))
        hidden = (preact * cdf).astype(jnp.bfloat16)
        hidden_ref[:, at : at + STEP] = hidden
        slope_ref[:, at : at + STEP] = cdf + preact * dens
        put_pieces(spread, mm(down_t, hidden), at)
    trade_leader(spread, 1)
    out_ref[...] = spread[...].astype(jnp.bfloat16)


def error_kernel(scale, in_ref, last_ref, teacher_ref, out_ref, grad_ref, spread_in, spread):
    take_in(spread_in, in_ref, 1)
    last = last_ref[0]
    last_t = last.T
    grad_last = None
    for at in range(0, teacher_ref.shape[1], STEP):
        returned = get_pieces(spread_in, at, STEP)
        teacher = teacher_ref[:, at : at + STEP].astype(jnp.float32)
        err = ((mm(last_t, returned) - teacher) * scale).astype(jnp.bfloat16)
        put_pieces(spread, mm(last, err), at)
        part = dot(returned, err, ((1,), (1,)))
        grad_last = part if grad_last is None else grad_last + part
    trade_leader(spread, 2)
    out_ref[...] = spread[...].astype(jnp.bfloat16)
    grad_ref[...] = grad_last


def backward_kernel(
    in_ref, down_ref, up_t_ref, slope_ref, hidden_ref, arrived_ref, last_ref,
    out_hbm, mine_ref, theirs_ref, spread_in, spread, buffer, sems,
):
    units, count = hidden_ref.shape
    half = units // 2
    take_in(spread_in, in_ref, 2)
    grad_out = get_pieces(spread_in, 0, count)
    grad_hidden = mm(down_ref[...], grad_out)
    grad = (grad_hidden * slope_ref[...]).astype(jnp.bfloat16)
    put_pieces(spread, mm(up_t_ref[...], grad), 0)
    copies = send_out(spread, buffer, out_hbm, sems, 0, 3)
    mine_ref[units:, :] = last_ref[...]
    theirs_ref[units:, :] = last_ref[...]
    down = dot(hidden_ref[...], grad_out, ((1,), (1,)))
    mine_ref[half:units, :] = down[:half]
    theirs_ref[half:units, :] = down[half:]
    take_in(spread_in, arrived_ref, 0)
    up = dot(grad, get_pieces(spread_in, 0, count), ((1,), (1,)))
    mine_ref[0:half, :] = up[:half]
    theirs_ref[0:half, :] = up[half:]
    for copy in copies:
        copy.wait()


def chip_sum_kernel(mine_ref, got_ref, mine_out, theirs_out):
    quarter = (mine_ref.shape[0] - BS) // 4
    total = mine_ref[...] + got_ref[...]
    last = total[4 * quarter :].astype(jnp.bfloat16)
    mine_out[0:quarter, :] = total[0:quarter]
    theirs_out[0:quarter, :] = total[quarter : 2 * quarter].astype(jnp.bfloat16)
    mine_out[quarter : 2 * quarter, :] = total[2 * quarter : 3 * quarter]
    theirs_out[quarter : 2 * quarter, :] = total[3 * quarter : 4 * quarter].astype(jnp.bfloat16)
    mine_out[2 * quarter :, :] = last.astype(jnp.float32)
    theirs_out[2 * quarter :, :] = last


def totals_kernel(mine_ref, got_ref, mix_ref, up_ref, down_ref, last_ref):
    quarter = up_ref.shape[1]
    total = mine_ref[...] + got_ref[...].astype(jnp.float32)
    ids = lax.broadcasted_iota(jnp.int32, (BS, BS), 0)
    one_hot = (mix_ref[...] == ids).astype(jnp.float32)
    up_ref[0] = jnp.dot(
        total[0:quarter], one_hot, precision=lax.Precision.HIGHEST, preferred_element_type=jnp.float32
    )
    down_ref[0] = total[quarter : 2 * quarter]
    last_ref[0] = total[2 * quarter :]


def last_kernel(in_ref, x_ref, out_ref, spread_in):
    take_in(spread_in, in_ref, 3)
    grad = get_pieces(spread_in, 0, x_ref.shape[0])
    out_ref[...] = mm(grad, x_ref[...]).T.astype(jnp.bfloat16)


VMEM = pl.BlockSpec(memory_space=pltpu.VMEM)
HBM = pl.BlockSpec(memory_space=pltpu.HBM)
BF16 = jnp.bfloat16
F32 = jnp.float32


def call(kernel, ins, outs, scratch, flops, in_specs=None, out_specs=None, pin=True):
    moved = sum(a.size * a.dtype.itemsize for a in ins) + sum(
        math.prod(o.shape) * o.dtype.itemsize for o in outs
    )
    if in_specs:
        ins = [
            pltpu.with_memory_space_constraint(a, pltpu.HBM) if spec is HBM else a
            for a, spec in zip(ins, in_specs)
        ]
    places = out_specs or [VMEM] * len(outs)
    if pin:
        outs = tuple(
            (pltpu.HBM if spec is HBM else pltpu.VMEM)(o.shape, o.dtype) for o, spec in zip(outs, places)
        )
    return pl.pallas_call(
        kernel,
        out_shape=outs,
        in_specs=in_specs or [VMEM] * len(ins),
        out_specs=out_specs or [VMEM] * len(outs),
        scratch_shapes=scratch,
        compiler_params=pltpu.CompilerParams(vmem_limit_bytes=16 * 1024 * 1024),
        cost_estimate=pl.CostEstimate(flops=flops, bytes_accessed=moved, transcendentals=0),
    )(*ins)


def local(inputs, targets, row_order, mix_order, first_factor, up_factor, down_factor, last_factor):
    tokens = inputs.shape[0]
    count = tokens // N_HID
    steps = count // STEP
    piece_rows = BS * count // LANES
    loss_scale = 1.0 / math.sqrt(tokens)
    quarter_units = up_factor.shape[1]
    units = quarter_units * N_HID
    mix_row = mix_order[None, :]
    shape = jax.ShapeDtypeStruct
    pieces = shape((piece_rows, LANES), BF16)
    spread = pltpu.VMEM((piece_rows, LANES), F32)
    buffer = pltpu.VMEM((piece_rows, LANES), BF16)
    flops = 2 * units * BS * count
    small = 2 * BS * BS * count
    two_sems = pltpu.SemaphoreType.DMA((2,))

    first_out, weights, x_own, rows = call(
        first_kernel,
        (inputs, first_factor, up_factor, down_factor, row_order.reshape(-1, LANES)),
        (
            pieces,
            shape((2 * quarter_units, BS), BF16),
            shape((count, BS), BF16),
            shape((count // LANES, LANES), jnp.int32),
        ),
        [
            pltpu.VMEM((count, BS), BF16),
            pltpu.VMEM((1, BS, BS), BF16),
            pltpu.VMEM((2 * quarter_units, BS), BF16),
            pltpu.VMEM((count // LANES, LANES), jnp.int32),
            spread,
            buffer,
            pltpu.SemaphoreType.DMA((10,)),
        ],
        small,
        [HBM] * 5,
        [HBM] * 4,
    )
    far = from_partner(weights, 2)
    arrived = exchange(first_out, 0)

    teacher = targets.at[rows.reshape(count)].get(mode="promise_in_bounds", wrap_negative_indices=False)
    weights, far, teacher = lax.optimization_barrier((weights, far, teacher))
    near, other = from_partner(weights, 1), from_partner(far, 1)
    (teacher_t,) = call(turn_kernel, (teacher,), (shape((BS, count), BF16),), [], small)
    up_mixed, down_t, up_mixed_t, down = call(
        prepare_kernel,
        (weights, far, near, other, mix_row),
        (
            shape((units, BS), BF16),
            shape((BS, units), BF16),
            shape((BS, units), BF16),
            shape((units, BS), BF16),
        ),
        [pltpu.VMEM((BS, units), BF16), pltpu.VMEM((units, BS), BF16), two_sems],
        small,
        out_specs=[VMEM, VMEM, HBM, HBM],
    )
    teacher_t, arrived = lax.optimization_barrier((teacher_t, arrived))

    summed, slope, hidden = call(
        forward_kernel,
        (arrived, up_mixed, down_t),
        (pieces, shape((units, count), F32), shape((units, count), BF16)),
        [spread, spread],
        2 * flops,
    )
    returned = exchange(summed, 1)

    grad_returned, grad_last = call(
        functools.partial(error_kernel, loss_scale),
        (returned, last_factor, teacher_t),
        (pieces, shape((BS, BS), F32)),
        [spread, spread],
        3 * small,
    )
    grad_arrived = exchange(grad_returned, 2)

    half_rows = shape((units + BS, BS), F32)
    grad_grouped, mine, theirs = call(
        backward_kernel,
        (grad_arrived, down, up_mixed_t, slope, hidden, arrived, grad_last),
        (pieces, half_rows, half_rows),
        [spread, spread, buffer, two_sems],
        4 * flops,
        out_specs=[HBM, VMEM, VMEM],
    )
    grad_first_out = exchange(grad_grouped, 3)

    quarter_rows = shape((units // 2 + BS, BS), F32)
    sent_rows = shape((units // 2 + BS, BS), BF16)
    mine, theirs = call(
        chip_sum_kernel, (mine, from_partner(theirs, 1)), (quarter_rows, sent_rows), [], 0
    )
    factor_grad = shape((1, quarter_units, BS), F32)
    grad_up, grad_down, grad_last = call(
        totals_kernel,
        (mine, from_partner(theirs, 2), mix_row),
        (factor_grad, factor_grad, shape((1, BS, BS), F32)),
        [],
        0,
        pin=False,
    )

    (grad_first,) = call(
        last_kernel, (grad_first_out, x_own), (shape((BS, BS), BF16),), [spread], small
    )
    grad_first = sum_over_hid(grad_first)
    return (grad_first[None], grad_up, grad_down, grad_last)


def solution(mesh):
    placed = (
        P(None, "blk"),
        P(None, "blk"),
        P(),
        P(),
        P("blk", None, None),
        P("blk", "hid", None),
        P("blk", "hid", None),
        P("blk", None, None),
    )
    return jax.shard_map(
        local,
        mesh=mesh,
        in_specs=placed,
        out_specs=(
            P("blk", None, None),
            P("blk", "hid", None),
            P("blk", "hid", None),
            P("blk", None, None),
        ),
        check_vma=False,
    )
```

```python
import functools
import math

import jax
import jax.numpy as jnp
from jax import lax
from jax.experimental import pallas as pl
from jax.experimental.pallas import tpu as pltpu
from jax.sharding import PartitionSpec as P

BS = 128
NB = 64
N_HID = 4
LANES = 128
STEP = 1024
LEADERS = (45, 53, 53, 53)


def token_groups(leader):
    order = list(range(NB))
    order[0], order[leader] = leader, 0
    return [[b * N_HID + (q ^ (2 * (b % 2))) for b in order] for q in range(N_HID)]


def from_partner(value, m):
    return lax.ppermute(value, "hid", [(i, i ^ m) for i in range(N_HID)])


def exchange(rows, step):
    pieces = rows.reshape(NB, rows.shape[0] // NB, LANES)
    pieces = lax.all_to_all(
        pieces, ("blk", "hid"), 0, 0, tiled=True, axis_index_groups=token_groups(LEADERS[step])
    )
    return pieces.reshape(rows.shape)


def dot(a, b, dims):
    return lax.dot_general(a, b, (dims, ((), ())), preferred_element_type=jnp.float32)


def mm(a, b):
    return dot(a, b, ((1,), (0,)))


def sum_over_hid(part):
    got = [from_partner(part, m).astype(jnp.float32) for m in (1, 2, 3)]
    return (part.astype(jnp.float32) + got[0]) + (got[1] + got[2])


def own_quarter():
    return lax.axis_index("hid") ^ (2 * (lax.axis_index("blk") % 2))


def put_pieces(spread, value, at):
    chunks = spread.shape[0] // BS
    for j in range(value.shape[1] // LANES):
        spread[pl.ds(at // LANES + j, BS, chunks), :] = value[:, j * LANES : (j + 1) * LANES]


def get_pieces(spread, at, size):
    chunks = spread.shape[0] // BS
    parts = [spread[pl.ds(at // LANES + j, BS, chunks), :] for j in range(size // LANES)]
    return jnp.concatenate(parts, axis=1).astype(jnp.bfloat16)


def trade_leader(spread, step):
    size = spread.shape[0] // NB
    at = LEADERS[step] * size
    leader = spread[at : at + size, :]
    spread[at : at + size, :] = spread[0:size, :]
    spread[0:size, :] = leader


def take_in(spread, ref, step):
    spread[...] = ref[...].astype(jnp.float32)
    trade_leader(spread, step)


def send_out(spread, buffer, hbm, sems, first_sem, step):
    trade_leader(spread, step)
    half = spread.shape[0] // 2
    copies = []
    for i in range(2):
        rows = pl.ds(i * half, half)
        buffer[rows, :] = spread[rows, :].astype(jnp.bfloat16)
        copies.append(pltpu.make_async_copy(buffer.at[rows], hbm.at[rows], sems.at[first_sem + i]))
        copies[-1].start()
    return copies


def first_kernel(
    x_hbm, first_hbm, up_hbm, down_hbm, order_hbm, out_hbm, packed_hbm, rows_hbm,
    x, first, packed, rows, spread, buffer, sems,
):
    count = x.shape[0]
    units = up_hbm.shape[1]
    order_rows = rows.shape[0]
    start = pl.multiple_of(own_quarter() * count, count)
    order_start = pl.multiple_of(own_quarter() * order_rows, order_rows)
    fetch = [
        (x_hbm.at[pl.ds(start, count)], x),
        (first_hbm, first),
        (up_hbm.at[0], packed.at[pl.ds(0, units)]),
        (down_hbm.at[0], packed.at[pl.ds(units, units)]),
        (order_hbm.at[pl.ds(order_start, order_rows)], rows),
    ]
    fetch = [pltpu.make_async_copy(a, b, sems.at[i]) for i, (a, b) in enumerate(fetch)]
    for copy in fetch:
        copy.start()
    fetch[1].wait()
    first_t = first[0].T
    fetch[0].wait()
    put_pieces(spread, dot(first_t, x[...], ((1,), (1,))), 0)
    copies = send_out(spread, buffer, out_hbm, sems, 5, 0)
    for copy in fetch[2:]:
        copy.wait()
    for i, (source, target) in enumerate(((packed, packed_hbm), (rows, rows_hbm))):
        copies.append(pltpu.make_async_copy(source, target, sems.at[7 + i]))
        copies[-1].start()
    for copy in copies:
        copy.wait()


def own_rows_kernel(x_hbm, out_ref, sem):
    count = out_ref.shape[0]
    start = pl.multiple_of(own_quarter() * count, count)
    copy = pltpu.make_async_copy(x_hbm.at[pl.ds(start, count)], out_ref, sem)
    copy.start()
    copy.wait()


def unit_matrix():
    ids = lax.broadcasted_iota(jnp.int32, (BS, BS), 0)
    eye = (lax.broadcasted_iota(jnp.int32, (BS, BS), 1) == ids).astype(jnp.float32)
    return eye.astype(jnp.bfloat16)


def prepare_kernel(
    own_ref, far_ref, near_ref, other_ref, mix_ref, up_ref, down_t_ref, up_t_hbm, down_hbm, up_t, down, sems
):
    units = own_ref.shape[0] // 2
    refs = (own_ref, far_ref, near_ref, other_ref)
    ids = lax.broadcasted_iota(jnp.int32, (BS, BS), 0)
    one_hot = (mix_ref[...] == ids).astype(jnp.float32).astype(jnp.bfloat16)
    for i, ref in enumerate(refs):
        down[i * units : (i + 1) * units, :] = ref[units:, :]
    copies = [pltpu.make_async_copy(down, down_hbm, sems.at[0])]
    copies[0].start()
    up = jnp.concatenate([ref[0:units, :] for ref in refs])
    up_t[...] = dot(one_hot, up, ((1,), (1,))).astype(jnp.bfloat16)
    copies.append(pltpu.make_async_copy(up_t, up_t_hbm, sems.at[1]))
    copies[1].start()
    up_ref[...] = dot(up, one_hot, ((1,), (1,))).astype(jnp.bfloat16)
    down_t_ref[...] = dot(unit_matrix(), down[...], ((1,), (1,))).astype(jnp.bfloat16)
    for copy in copies:
        copy.wait()


def turn_kernel(in_ref, out_ref):
    out_ref[...] = dot(unit_matrix(), in_ref[...], ((1,), (1,))).astype(jnp.bfloat16)


def forward_kernel(
    in_ref, up_ref, down_t_ref, out_ref, slope_ref, hidden_ref, spread_in, spread
):
    take_in(spread_in, in_ref, 0)
    up = up_ref[...]
    down_t = down_t_ref[...]
    for at in range(0, hidden_ref.shape[1], STEP):
        preact = mm(up, get_pieces(spread_in, at, STEP))
        cdf = 0.5 * (1.0 + lax.erf(preact * (1.0 / math.sqrt(2.0))))
        dens = jnp.exp(-0.5 * preact * preact) * (1.0 / math.sqrt(2.0 * math.pi))
        hidden = (preact * cdf).astype(jnp.bfloat16)
        hidden_ref[:, at : at + STEP] = hidden
        slope_ref[:, at : at + STEP] = cdf + preact * dens
        put_pieces(spread, mm(down_t, hidden), at)
    trade_leader(spread, 1)
    out_ref[...] = spread[...].astype(jnp.bfloat16)


def error_kernel(scale, in_ref, last_ref, teacher_ref, out_ref, grad_ref, spread_in, spread):
    take_in(spread_in, in_ref, 1)
    last = last_ref[0]
    last_t = last.T
    grad_last = None
    for at in range(0, teacher_ref.shape[1], STEP):
        returned = get_pieces(spread_in, at, STEP)
        teacher = teacher_ref[:, at : at + STEP].astype(jnp.float32)
        err = ((mm(last_t, returned) - teacher) * scale).astype(jnp.bfloat16)
        put_pieces(spread, mm(last, err), at)
        part = dot(returned, err, ((1,), (1,)))
        grad_last = part if grad_last is None else grad_last + part
    trade_leader(spread, 2)
    out_ref[...] = spread[...].astype(jnp.bfloat16)
    grad_ref[...] = grad_last


def backward_kernel(
    in_ref, down_ref, up_t_ref, slope_ref, hidden_ref, arrived_ref, last_ref,
    out_hbm, mine_ref, theirs_ref, spread_in, spread, buffer, sems,
):
    units, count = hidden_ref.shape
    half = units // 2
    take_in(spread_in, in_ref, 2)
    grad_out = get_pieces(spread_in, 0, count)
    grad_hidden = mm(down_ref[...], grad_out)
    grad = (grad_hidden * slope_ref[...]).astype(jnp.bfloat16)
    put_pieces(spread, mm(up_t_ref[...], grad), 0)
    copies = send_out(spread, buffer, out_hbm, sems, 0, 3)
    mine_ref[units:, :] = last_ref[...]
    theirs_ref[units:, :] = last_ref[...]
    down = dot(hidden_ref[...], grad_out, ((1,), (1,)))
    mine_ref[half:units, :] = down[:half]
    theirs_ref[half:units, :] = down[half:]
    take_in(spread_in, arrived_ref, 0)
    up = dot(grad, get_pieces(spread_in, 0, count), ((1,), (1,)))
    mine_ref[0:half, :] = up[:half]
    theirs_ref[0:half, :] = up[half:]
    for copy in copies:
        copy.wait()


def chip_sum_kernel(mine_ref, got_ref, mine_out, theirs_out):
    quarter = (mine_ref.shape[0] - BS) // 4
    total = mine_ref[...] + got_ref[...]
    last = total[4 * quarter :].astype(jnp.bfloat16)
    mine_out[0:quarter, :] = total[0:quarter]
    theirs_out[0:quarter, :] = total[quarter : 2 * quarter].astype(jnp.bfloat16)
    mine_out[quarter : 2 * quarter, :] = total[2 * quarter : 3 * quarter]
    theirs_out[quarter : 2 * quarter, :] = total[3 * quarter : 4 * quarter].astype(jnp.bfloat16)
    mine_out[2 * quarter :, :] = last.astype(jnp.float32)
    theirs_out[2 * quarter :, :] = last


def totals_kernel(mine_ref, got_ref, mix_ref, up_ref, down_ref, last_ref):
    quarter = up_ref.shape[1]
    total = mine_ref[...] + got_ref[...].astype(jnp.float32)
    ids = lax.broadcasted_iota(jnp.int32, (BS, BS), 0)
    one_hot = (mix_ref[...] == ids).astype(jnp.float32)
    up_ref[0] = jnp.dot(
        total[0:quarter], one_hot, precision=lax.Precision.HIGHEST, preferred_element_type=jnp.float32
    )
    down_ref[0] = total[quarter : 2 * quarter]
    last_ref[0] = total[2 * quarter :]


def last_kernel(in_ref, x_ref, out_ref, spread_in):
    take_in(spread_in, in_ref, 3)
    grad = get_pieces(spread_in, 0, x_ref.shape[0])
    out_ref[...] = mm(grad, x_ref[...]).T.astype(jnp.bfloat16)


VMEM = pl.BlockSpec(memory_space=pltpu.VMEM)
HBM = pl.BlockSpec(memory_space=pltpu.HBM)
BF16 = jnp.bfloat16
F32 = jnp.float32


def call(kernel, ins, outs, scratch, flops, in_specs=None, out_specs=None, pin=True):
    moved = sum(a.size * a.dtype.itemsize for a in ins) + sum(
        math.prod(o.shape) * o.dtype.itemsize for o in outs
    )
    if in_specs:
        ins = [
            pltpu.with_memory_space_constraint(a, pltpu.HBM) if spec is HBM else a
            for a, spec in zip(ins, in_specs)
        ]
    places = out_specs or [VMEM] * len(outs)
    if pin:
        outs = tuple(
            (pltpu.HBM if spec is HBM else pltpu.VMEM)(o.shape, o.dtype) for o, spec in zip(outs, places)
        )
    return pl.pallas_call(
        kernel,
        out_shape=outs,
        in_specs=in_specs or [VMEM] * len(ins),
        out_specs=out_specs or [VMEM] * len(outs),
        scratch_shapes=scratch,
        compiler_params=pltpu.CompilerParams(vmem_limit_bytes=16 * 1024 * 1024),
        cost_estimate=pl.CostEstimate(flops=flops, bytes_accessed=moved, transcendentals=0),
    )(*ins)


def local(inputs, targets, row_order, mix_order, first_factor, up_factor, down_factor, last_factor):
    tokens = inputs.shape[0]
    count = tokens // N_HID
    steps = count // STEP
    piece_rows = BS * count // LANES
    loss_scale = 1.0 / math.sqrt(tokens)
    quarter_units = up_factor.shape[1]
    units = quarter_units * N_HID
    mix_row = mix_order[None, :]
    shape = jax.ShapeDtypeStruct
    pieces = shape((piece_rows, LANES), BF16)
    spread = pltpu.VMEM((piece_rows, LANES), F32)
    buffer = pltpu.VMEM((piece_rows, LANES), BF16)
    flops = 2 * units * BS * count
    small = 2 * BS * BS * count
    two_sems = pltpu.SemaphoreType.DMA((2,))

    first_out, weights, rows = call(
        first_kernel,
        (inputs, first_factor, up_factor, down_factor, row_order.reshape(-1, LANES)),
        (
            pieces,
            shape((2 * quarter_units, BS), BF16),
            shape((count // LANES, LANES), jnp.int32),
        ),
        [
            pltpu.VMEM((count, BS), BF16),
            pltpu.VMEM((1, BS, BS), BF16),
            pltpu.VMEM((2 * quarter_units, BS), BF16),
            pltpu.VMEM((count // LANES, LANES), jnp.int32),
            spread,
            buffer,
            pltpu.SemaphoreType.DMA((9,)),
        ],
        small,
        [HBM] * 5,
        [HBM] * 3,
    )
    far = from_partner(weights, 2)
    arrived = exchange(first_out, 0)

    teacher = targets.at[rows.reshape(count)].get(mode="promise_in_bounds", wrap_negative_indices=False)
    weights, far, teacher = lax.optimization_barrier((weights, far, teacher))
    near, other = from_partner(weights, 1), from_partner(far, 1)
    (teacher_t,) = call(turn_kernel, (teacher,), (shape((BS, count), BF16),), [], small)
    up_mixed, down_t, up_mixed_t, down = call(
        prepare_kernel,
        (weights, far, near, other, mix_row),
        (
            shape((units, BS), BF16),
            shape((BS, units), BF16),
            shape((BS, units), BF16),
            shape((units, BS), BF16),
        ),
        [pltpu.VMEM((BS, units), BF16), pltpu.VMEM((units, BS), BF16), two_sems],
        small,
        out_specs=[VMEM, VMEM, HBM, HBM],
    )
    teacher_t, arrived = lax.optimization_barrier((teacher_t, arrived))

    summed, slope, hidden = call(
        forward_kernel,
        (arrived, up_mixed, down_t),
        (pieces, shape((units, count), F32), shape((units, count), BF16)),
        [spread, spread],
        2 * flops,
    )
    returned = exchange(summed, 1)

    grad_returned, grad_last = call(
        functools.partial(error_kernel, loss_scale),
        (returned, last_factor, teacher_t),
        (pieces, shape((BS, BS), F32)),
        [spread, spread],
        3 * small,
    )
    grad_arrived = exchange(grad_returned, 2)

    half_rows = shape((units + BS, BS), F32)
    grad_grouped, mine, theirs = call(
        backward_kernel,
        (grad_arrived, down, up_mixed_t, slope, hidden, arrived, grad_last),
        (pieces, half_rows, half_rows),
        [spread, spread, buffer, two_sems],
        4 * flops,
        out_specs=[HBM, VMEM, VMEM],
    )
    grad_first_out = exchange(grad_grouped, 3)

    quarter_rows = shape((units // 2 + BS, BS), F32)
    sent_rows = shape((units // 2 + BS, BS), BF16)
    got = from_partner(theirs, 1)
    inputs, got = lax.optimization_barrier((inputs, got))
    (x_own,) = call(
        own_rows_kernel, (inputs,), (shape((count, BS), BF16),), [pltpu.SemaphoreType.DMA], 0, [HBM]
    )
    mine, theirs = call(chip_sum_kernel, (mine, got), (quarter_rows, sent_rows), [], 0)
    factor_grad = shape((1, quarter_units, BS), F32)
    grad_up, grad_down, grad_last = call(
        totals_kernel,
        (mine, from_partner(theirs, 2), mix_row),
        (factor_grad, factor_grad, shape((1, BS, BS), F32)),
        [],
        0,
        pin=False,
    )

    (grad_first,) = call(
        last_kernel, (grad_first_out, x_own), (shape((BS, BS), BF16),), [spread], small
    )
    grad_first = sum_over_hid(grad_first)
    return (grad_first[None], grad_up, grad_down, grad_last)


def solution(mesh):
    placed = (
        P(None, "blk"),
        P(None, "blk"),
        P(),
        P(),
        P("blk", None, None),
        P("blk", "hid", None),
        P("blk", "hid", None),
        P("blk", None, None),
    )
    return jax.shard_map(
        local,
        mesh=mesh,
        in_specs=placed,
        out_specs=(
            P("blk", None, None),
            P("blk", "hid", None),
            P("blk", "hid", None),
            P("blk", None, None),
        ),
        check_vma=False,
    )
```
